512 devices in a mesh: slab: 32 (over y, z_lo), row: 16 (over z_hi, x, core).
Axes of the slice: x: 4, y: 4, z: 16 (z_hi: 2, z_lo: 8; z = z_hi * 8 + z_lo), core: 2. Of those that a mesh axis runs over, the one named last changes fastest.
Arguments:
- queries: bfloat16 [32768, 32, 128], P('slab', 'row'), may hold values from -72 to 72, as said below
- keys: bfloat16 [32768, 32, 128], P('slab', 'row'), may hold values from -4 to 4
- values: bfloat16 [32768, 32, 128], P('slab', 'row'), may hold values from -6 to 6
- out_grad: bfloat16 [32768, 32, 128], P(('slab', 'row')), may hold values from -6 to 6
- col_start: int32 [256], replicated, may hold values from 0 to 2, as said below
- valid_tiles: int32 [32], replicated, may hold values from 4 to 8, as said below
Outputs:
- query_grad: bfloat16 [32768, 32, 128], P(('slab', 'row'))
- key_grad: bfloat16 [32768, 32, 128], P(('slab', 'row'))
- value_grad: bfloat16 [32768, 32, 128], P(('slab', 'row'))
The draws below stay inside these ranges and needn't reach their ends.
Inputs may be any that keep to these rules, and one draw needn't show every extreme that they name: `queries`: of order one in most rows. For query tile a with tile column w = (a % 8) % 4, col_start[a] is w - 1 or w, kept within 0 to 2. The tiles of a slab with index below valid_tiles hold real keys, the others padding; the values 4 and 8 occur in every draw.
All inputs are finite; a program needn't handle non-finite values.
Results may differ from the reference program's by a relative error of at most 0.0095.
Values may be sent and summed in bfloat16 or wider, within the bound.
A program may use at most 128 MiB of HBM per device.

```python
import jax
import jax.numpy as jnp
from jax import lax

HEADS = 32
HD = 128
TILE = 128
GH = 2
GW = 4
WIN_COLS = 2
TPS = 8
SLABS = 32
TILES = 256
TOKENS = 32768


def keys_common(key):
    raw_keys = jnp.clip(jax.random.normal(jax.random.fold_in(key, 11), (TOKENS, HEADS, HD), jnp.float32), -3.5, 3.5)
    return raw_keys


def draw_keys(key, part):
    raw_keys = keys_common(key)
    return raw_keys.astype(jnp.bfloat16)


def draw_queries(key, part):
    drawn = jnp.clip(jax.random.normal(jax.random.fold_in(key, 13), (TOKENS, HEADS, HD), jnp.float32), -3.5, 3.5)
    return drawn.astype(jnp.bfloat16)


def draw_col_start(key, part):
    tile_ids = jnp.arange(TILES, dtype=jnp.int32)
    column = tile_ids % GW
    backward = jax.random.randint(jax.random.fold_in(key, 21), (TILES,), 0, 2, jnp.int32)
    return jnp.clip(column - backward, 0, GW - WIN_COLS).astype(jnp.int32)


def draw_valid_tiles(key, part):
    counts = jax.random.randint(jax.random.fold_in(key, 31), (SLABS,), GW, GH * GW + 1, jnp.int32)
    fuller = jax.random.randint(jax.random.fold_in(key, 32), (), 0, SLABS, jnp.int32)
    emptier = (fuller + 1 + jax.random.randint(jax.random.fold_in(key, 33), (), 0, SLABS - 1, jnp.int32)) % SLABS
    slab_ids = jnp.arange(SLABS, dtype=jnp.int32)
    counts = jnp.where(slab_ids == fuller, GH * GW, counts)
    counts = jnp.where(slab_ids == emptier, GW, counts)
    return counts.astype(jnp.int32)


def levels(key, shape, split, low, largest):
    def one(dim, blocks):
        draws = jax.random.uniform(jax.random.fold_in(jax.random.fold_in(key, 6), dim), (blocks,), jnp.float32, low / len(split), largest / len(split))
        return jnp.repeat(jnp.exp(draws), shape[dim] // blocks).reshape((-1,) + (1,) * (len(shape) - dim - 1))

    level = one(*split[0])
    for cut in split[1:]:
        level = level * one(*cut)
    return level


def scatter_about(stream_key, shape, deviation, bound, shards=(), kind=jnp.bfloat16):
    level = levels(stream_key, shape, shards, -0.22, 0.18) if shards else 1.0
    result = jax.random.normal(stream_key, shape, jnp.float32) * deviation * level
    return jnp.minimum(jnp.maximum(result, -bound), bound).astype(kind)


def setup_inputs(seed: int = 0) -> dict:
    key_of = jax.random.split(jax.random.key(seed), 7)
    queries = draw_queries(jax.random.fold_in(key_of[6], 71), 0)
    keys = draw_keys(jax.random.fold_in(key_of[6], 71), 0)
    values = scatter_about(key_of[2], (TOKENS, HEADS, HD), 1.0, 6.0, ((0, 32), (1, 16)))
    out_grad = scatter_about(key_of[3], (TOKENS, HEADS, HD), 1.0, 6.0, ((0, 512),))
    col_start = draw_col_start(jax.random.fold_in(key_of[6], 71), 0)
    valid_tiles = draw_valid_tiles(jax.random.fold_in(key_of[6], 71), 0)
    return dict(queries=queries, keys=keys, values=values, out_grad=out_grad, col_start=col_start, valid_tiles=valid_tiles)


def window_tiles(col_first, slab_pos, valid_tiles):
    per_row = GH * WIN_COLS
    slot_ids = jnp.arange(3 * per_row, dtype=jnp.int32)
    slab_step = slot_ids // per_row
    inner_slot = slot_ids % per_row
    tile_base = slab_step * TPS + (inner_slot // WIN_COLS) * GW + inner_slot % WIN_COLS
    key_tiles = tile_base[None, :] + col_first[:, None]
    key_slab = slab_pos - 1 + slab_step
    slab_ids = jnp.arange(SLABS, dtype=jnp.int32)
    counts = jnp.sum(jnp.where(slab_ids[None, :] == key_slab[:, None], valid_tiles[None, :], 0), axis=1)
    key_valid = (key_slab[None, :] >= 0) & (key_slab[None, :] < SLABS) & (key_tiles - slab_step[None, :] * TPS < counts[None, :])
    return key_tiles, key_valid


def reference(queries, keys, values, out_grad, col_start, valid_tiles):
    tok_slab = TPS * TILE
    inv_root = HD ** -0.5
    padding = jnp.zeros((tok_slab, HEADS, HD), keys.dtype)
    keys_padded = jnp.concatenate([padding, keys, padding], axis=0)
    values_padded = jnp.concatenate([padding, values, padding], axis=0)

    def slab_body(running, slab_pos):
        key_sums, value_sums = running
        row_start = slab_pos * tok_slab
        query_block = lax.dynamic_slice_in_dim(queries, row_start, tok_slab, 0).astype(jnp.float32).reshape(TPS, TILE, HEADS, HD)
        grad_rows = lax.dynamic_slice_in_dim(out_grad, row_start, tok_slab, 0).astype(jnp.float32).reshape(TPS, TILE, HEADS, HD)
        key_ext = lax.dynamic_slice_in_dim(keys_padded, row_start, 3 * tok_slab, 0).astype(jnp.float32).reshape(3 * TPS, TILE, HEADS, HD)
        value_ext = lax.dynamic_slice_in_dim(values_padded, row_start, 3 * tok_slab, 0).astype(jnp.float32).reshape(3 * TPS, TILE, HEADS, HD)
        col_first = lax.dynamic_slice_in_dim(col_start, slab_pos * TPS, TPS, 0)
        key_tiles, key_valid = window_tiles(col_first, slab_pos, valid_tiles)
        slot_count = key_tiles.shape[1]
        key_sel = key_ext[key_tiles].reshape(TPS, slot_count * TILE, HEADS, HD)
        value_sel = value_ext[key_tiles].reshape(TPS, slot_count * TILE, HEADS, HD)
        valid_wide = jnp.repeat(key_valid, TILE, axis=1)[:, None, None, :]
        scores = jnp.einsum('nqhd,nkhd->nhqk', query_block, key_sel) * inv_root
        scores = jnp.where(valid_wide, scores, -jnp.inf)
        row_max = jnp.max(scores, axis=-1, keepdims=True)
        expo_vals = jnp.exp(scores - row_max)
        attend = expo_vals / jnp.sum(expo_vals, axis=-1, keepdims=True)
        attend_b = lax.optimization_barrier(attend.astype(jnp.bfloat16)).astype(jnp.float32)
        output = jnp.einsum('nhqk,nkhd->nqhd', attend_b, value_sel)
        row_delta = jnp.einsum('nqhd,nqhd->nhq', grad_rows, output)
        grad_attend = jnp.einsum('nqhd,nkhd->nhqk', grad_rows, value_sel)
        grad_scores = lax.optimization_barrier((attend * (grad_attend - row_delta[..., None])).astype(jnp.bfloat16)).astype(jnp.float32)
        query_grad = jnp.einsum('nhqk,nkhd->nqhd', grad_scores, key_sel) * inv_root
        key_grad = jnp.einsum('nhqk,nqhd->nkhd', grad_scores, query_block) * inv_root
        value_grad = jnp.einsum('nhqk,nqhd->nkhd', attend_b, grad_rows)
        tile_shape = (TPS, slot_count, TILE, HEADS, HD)
        key_part = jnp.zeros((3 * TPS, TILE, HEADS, HD), jnp.float32).at[key_tiles].add(key_grad.reshape(tile_shape))
        value_part = jnp.zeros((3 * TPS, TILE, HEADS, HD), jnp.float32).at[key_tiles].add(value_grad.reshape(tile_shape))
        key_sums = lax.dynamic_update_slice_in_dim(key_sums, lax.dynamic_slice_in_dim(key_sums, row_start, 3 * tok_slab, 0) + key_part.reshape(3 * tok_slab, HEADS, HD), row_start, 0)
        value_sums = lax.dynamic_update_slice_in_dim(value_sums, lax.dynamic_slice_in_dim(value_sums, row_start, 3 * tok_slab, 0) + value_part.reshape(3 * tok_slab, HEADS, HD), row_start, 0)
        return (key_sums, value_sums), query_grad.reshape(tok_slab, HEADS, HD)

    zero_sums = jnp.zeros(((SLABS + 2) * tok_slab, HEADS, HD), jnp.float32)
    (key_sums, value_sums), query_rows = lax.scan(slab_body, (zero_sums, zero_sums), jnp.arange(SLABS, dtype=jnp.int32))
    query_grad = query_rows.reshape(TOKENS, HEADS, HD).astype(jnp.bfloat16)
    key_grad = key_sums[tok_slab:tok_slab + TOKENS].astype(jnp.bfloat16)
    value_grad = value_sums[tok_slab:tok_slab + TOKENS].astype(jnp.bfloat16)
    return query_grad, key_grad, value_grad
```

```python
import functools

import jax
import jax.numpy as jnp
from jax import lax
from jax.experimental import pallas as pl
from jax.experimental.pallas import tpu as pltpu
from jax.sharding import PartitionSpec as P

TILE = 128
GH = 2
GW = 4
WIN_COLS = 2
TPS = 8
NEG = -1e30
LOG2E = 1.4426950408889634


def attend_kernel(
    inv_root, cols_ref, counts_ref, q_ref, g_ref, own_ref, low_ref, high_ref,
    dq_ref, down_ref, dlow_ref, dhigh_ref, acc_ref,
):
    heads, tok_slab, _ = q_ref.shape
    span = WIN_COLS * TILE
    row_len = GW * TILE
    acc_ref[...] = jnp.zeros_like(acc_ref)
    sources = (low_ref, own_ref, high_ref)
    nt = (((1,), (1,)), ((), ()))
    tn = (((0,), (0,)), ((), ()))

    def step(index, carry):
        head = index // TPS
        tile = index % TPS
        rows = pl.ds(pl.multiple_of(tile * TILE, TILE), TILE)
        first = cols_ref[tile]
        query = q_ref[head, rows, :]
        grad = g_ref[head, rows, :]
        starts = []
        keys = []
        values = []
        bias = []
        for slab in range(3):
            for row in range(GH):
                start = pl.multiple_of(row * row_len + first * TILE, TILE)
                starts.append((slab, start))
                keys.append(sources[slab][0, head, pl.ds(start, span), :])
                values.append(sources[slab][1, head, pl.ds(start, span), :])
                for col in range(WIN_COLS):
                    valid = row * GW + first + col < counts_ref[slab]
                    bias.append(jnp.full((TILE, TILE), jnp.where(valid, 0.0, NEG), jnp.float32))
        keys = jnp.concatenate(keys, axis=0)
        values = jnp.concatenate(values, axis=0)
        bias = jnp.concatenate(bias, axis=0)
        scores = lax.dot_general(keys, query, nt, preferred_element_type=jnp.float32)
        scores = scores * (inv_root * LOG2E) + bias
        peak = jnp.max(scores, axis=0, keepdims=True)
        expo = jnp.exp2(scores - peak)
        total = jnp.sum(expo, axis=0, keepdims=True)
        attend = expo * (1.0 / total)
        attend_b = attend.astype(jnp.bfloat16)
        grad_attend = lax.dot_general(values, grad, nt, preferred_element_type=jnp.float32)
        delta = jnp.sum(attend_b.astype(jnp.float32) * grad_attend, axis=0, keepdims=True)
        grad_scores = (attend * (grad_attend - delta)).astype(jnp.bfloat16)
        dq = lax.dot_general(grad_scores, keys, tn, preferred_element_type=jnp.float32)
        dq_ref[head, rows, :] = (dq * inv_root).astype(dq_ref.dtype)
        dk = jnp.dot(grad_scores, query, preferred_element_type=jnp.float32)
        dv = jnp.dot(attend_b, grad, preferred_element_type=jnp.float32)
        for n, (slab, start) in enumerate(starts):
            acc_ref[0, head, slab, pl.ds(start, span), :] += dk[n * span : (n + 1) * span]
            acc_ref[1, head, slab, pl.ds(start, span), :] += dv[n * span : (n + 1) * span]
        return carry

    lax.fori_loop(0, heads * TPS, step, 0)
    for kv, scale in ((0, inv_root), (1, 1.0)):
        for head in range(heads):
            dlow_ref[kv, head] = (acc_ref[kv, head, 0] * scale).astype(dlow_ref.dtype)
            down_ref[kv, head] = acc_ref[kv, head, 1] * scale
            dhigh_ref[kv, head] = (acc_ref[kv, head, 2] * scale).astype(dhigh_ref.dtype)


def attend_call(cols, counts, query, grad, own, low, high):
    heads, tok_slab, head_dim = query.shape
    smem = pl.BlockSpec(memory_space=pltpu.SMEM)
    vmem = pl.BlockSpec(memory_space=pltpu.VMEM)
    pairs = heads * TPS * TILE * 3 * GH * WIN_COLS * TILE
    return pl.pallas_call(
        functools.partial(attend_kernel, head_dim ** (-0.5)),
        out_shape=(
            jax.ShapeDtypeStruct(query.shape, jnp.bfloat16),
            jax.ShapeDtypeStruct(own.shape, jnp.float32),
            jax.ShapeDtypeStruct(own.shape, jnp.bfloat16),
            jax.ShapeDtypeStruct(own.shape, jnp.bfloat16),
        ),
        in_specs=[smem, smem] + [vmem] * 5,
        out_specs=(vmem,) * 4,
        scratch_shapes=[pltpu.VMEM((2, heads, 3, tok_slab, head_dim), jnp.float32)],
        compiler_params=pltpu.CompilerParams(vmem_limit_bytes=48 * 2**20),
        cost_estimate=pl.CostEstimate(
            flops=10 * pairs * head_dim, bytes_accessed=8 * 2**20, transcendentals=pairs
        ),
    )(cols, counts, query, grad, own, low, high)


def on_device(queries, keys, values, out_grad, col_start, valid_tiles):
    slab_total = valid_tiles.shape[0]
    slab_pos = lax.axis_index("slab")
    forward = [(i, i + 1) for i in range(slab_total - 1)]
    backward = [(i + 1, i) for i in range(slab_total - 1)]
    grad = lax.all_to_all(out_grad, "row", split_axis=1, concat_axis=0, tiled=True)
    own = jnp.stack([keys, values]).swapaxes(1, 2)
    low = lax.ppermute(own, "slab", forward)
    high = lax.ppermute(own, "slab", backward)
    cols = lax.dynamic_slice_in_dim(col_start, slab_pos * TPS, TPS, 0)
    padded = jnp.pad(valid_tiles, 1)
    counts = lax.dynamic_slice_in_dim(padded, slab_pos, 3, 0)
    dq, down, dlow, dhigh = attend_call(
        cols, counts, queries.swapaxes(0, 1), grad.swapaxes(0, 1), own, low, high
    )
    from_high = lax.ppermute(dlow, "slab", backward)
    from_low = lax.ppermute(dhigh, "slab", forward)
    sums = down + from_high.astype(jnp.float32) + from_low.astype(jnp.float32)
    sums = sums.astype(jnp.bfloat16)

    def home(array):
        return lax.all_to_all(array.swapaxes(0, 1), "row", split_axis=0, concat_axis=1, tiled=True)

    return home(dq), home(sums[0]), home(sums[1])


def solution(mesh):
    head_split = P("slab", "row", None)
    token_split = P(("slab", "row"), None, None)
    return jax.shard_map(
        on_device,
        mesh=mesh,
        in_specs=(head_split, head_split, head_split, token_split, P(), P()),
        out_specs=(token_split,) * 3,
        check_vma=False,
    )
```

```python
import functools

import jax
import jax.numpy as jnp
from jax import lax
from jax.experimental import pallas as pl
from jax.experimental.pallas import tpu as pltpu
from jax.sharding import PartitionSpec as P

TILE = 128
GH = 2
GW = 4
WIN_COLS = 2
TPS = 8
NEG = -1e30
LOG2E = 1.4426950408889634
MESH = pl.DeviceIdType.MESH
NT = (((1,), (1,)), ((), ()))
TN = (((0,), (0,)), ((), ()))


def fused_kernel(
    slabs, rows, inv_root, shift_ref, bias_ref, q_ref, k_ref, v_ref, g_ref,
    oq_ref, okv_ref,
    q_side, g_own, g_side, expo_ref, gatt_ref, stat, stat_in, final, final_in,
    acc, kv_out, dq_own, dq_side, dq_in, dq_out,
    q_send, q_recv, a_send, a_recv, g_send, g_recv, s_send, s_recv, f_send, f_recv,
    kv_send, kv_recv, dq_send, dq_recv, o_send, o_recv,
):
    heads, tok_slab, head_dim = q_ref.shape
    block = g_ref.shape[1]
    span = WIN_COLS * TILE
    row_len = GW * TILE
    slab = lax.axis_index("slab")
    row = lax.axis_index("row")
    below = lax.rem(slab + slabs - 1, slabs)
    above = lax.rem(slab + 1, slabs)
    sides = (below, above)

    def peer(step):
        return lax.rem(row + step, rows)

    barrier = pltpu.get_barrier_semaphore()
    for side in sides:
        pl.semaphore_signal(barrier, inc=1, device_id=(side, row), device_id_type=MESH)

    def greet(step, carry):
        pl.semaphore_signal(barrier, inc=1, device_id=(slab, peer(step)), device_id_type=MESH)
        return carry

    lax.fori_loop(1, rows, greet, 0)
    pl.semaphore_wait(barrier, rows + 1)

    def to_side(src, dst, n, send, recv, head):
        return pltpu.make_async_remote_copy(
            src_ref=src,
            dst_ref=dst,
            send_sem=send.at[head, n],
            recv_sem=recv.at[head, 1 - n],
            device_id=(sides[n], row),
            device_id_type=MESH,
        )

    def from_side(ref, n, recv, head):
        pltpu.make_async_copy(ref, ref, recv.at[head, n]).wait()

    def all_sent(ref, sem):
        pltpu.make_async_copy(ref, ref, sem).wait()

    def send_queries(head):
        for n in range(2):
            to_side(q_ref.at[head], q_side.at[1 - n, head], n, q_send, q_recv, head).start()

    def spread_grad(head):
        def one(step, carry):
            other = peer(step)
            pltpu.make_async_remote_copy(
                src_ref=g_ref.at[other * heads + head],
                dst_ref=g_own.at[head, row],
                send_sem=a_send.at[head],
                recv_sem=a_recv.at[head],
                device_id=(slab, other),
                device_id_type=MESH,
            ).start()
            return carry

        lax.fori_loop(1, rows, one, 0)
        g_own[head, row] = g_ref[row * heads + head]

    def await_spread(buffer, send, recv, head):
        whole = buffer.at[pl.ds(0, rows - 1)]
        pltpu.make_async_copy(whole, whole, recv.at[head]).wait()
        pltpu.make_async_copy(whole, whole, send.at[head]).wait()

    def send_grads(head):
        for n in range(2):
            to_side(g_own.at[head], g_side.at[1 - n, head], n, g_send, g_recv, head).start()

    def pick(ref, head, tile, part):
        base = (tile % GW) // 2
        high = jnp.broadcast_to(shift_ref[part, pl.ds(tile, 1), :], (TILE, head_dim))
        high = high.astype(jnp.bfloat16)
        low = 1 - high
        chosen = []
        for r in range(GH):
            cols = [
                ref[head, pl.ds(pl.multiple_of((r * GW + base + c) * TILE, TILE), TILE), :]
                for c in range(WIN_COLS + 1)
            ]
            chosen += [cols[c] * low + cols[c + 1] * high for c in range(WIN_COLS)]
        return jnp.concatenate(chosen, axis=0)

    def query_of(head, tile, part):
        at = pl.ds(pl.multiple_of(tile * TILE, TILE), TILE)
        if part == 1:
            return q_ref[head, at, :]
        return q_side[part // 2, head, at, :]

    def grad_of(head, tile, part):
        each = TILE // block
        at = pl.ds(tile * each, each)
        if part == 1:
            return g_own[head, at].reshape(TILE, head_dim)
        return g_side[part // 2, head, at].reshape(TILE, head_dim)

    def first_pass(head, part):
        def one(tile, carry):
            keys = pick(k_ref, head, tile, part)
            values = pick(v_ref, head, tile, part)
            bias = jnp.concatenate(
                [
                    jnp.broadcast_to(bias_ref[n, part, pl.ds(tile, 1), :], (TILE, TILE))
                    for n in range(GH * WIN_COLS)
                ],
                axis=0,
            )
            scores = lax.dot_general(
                keys, query_of(head, tile, part), NT, preferred_element_type=jnp.float32
            )
            scores = scores * (inv_root * LOG2E) + bias
            peak = jnp.max(scores, axis=0, keepdims=True)
            expo = jnp.exp2(scores - peak)
            grad_attend = lax.dot_general(
                values, grad_of(head, tile, part), NT, preferred_element_type=jnp.float32
            )
            expo_ref[part, tile] = expo
            gatt_ref[part, tile] = grad_attend
            at = pl.ds(tile, 1)
            stat[head, part, 0, at, :] = peak
            stat[head, part, 1, at, :] = jnp.sum(expo, axis=0, keepdims=True)
            stat[head, part, 2, at, :] = jnp.sum(expo * grad_attend, axis=0, keepdims=True)
            return carry

        lax.fori_loop(0, TPS, one, 0)

    def send_stats(head):
        for n in range(2):
            to_side(
                stat.at[head, 2 * n], stat_in.at[1 - n, head], n, s_send, s_recv, head
            ).start()

    def combine(head):
        for n in range(2):
            from_side(stat_in.at[n, head], n, s_recv, head)
        peaks = [stat_in[0, head, 0], stat[head, 1, 0], stat_in[1, head, 0]]
        sums = [stat_in[0, head, 1], stat[head, 1, 1], stat_in[1, head, 1]]
        dots = [stat_in[0, head, 2], stat[head, 1, 2], stat_in[1, head, 2]]
        top = jnp.maximum(jnp.maximum(peaks[0], peaks[1]), peaks[2])
        weights = [jnp.exp2(p - top) for p in peaks]
        total = sum(w * s for w, s in zip(weights, sums))
        final[head, 0] = top
        final[head, 1] = 1.0 / total
        final[head, 2] = sum(w * d for w, d in zip(weights, dots)) / total
        for n in range(2):
            to_side(
                final.at[head], final_in.at[1 - n, head], n, f_send, f_recv, head
            ).start()

    def second_pass(head, part):
        def one(tile, carry):
            base = (tile % GW) // 2
            at = pl.ds(tile, 1)
            shifted = jnp.broadcast_to(shift_ref[part, at, :], (TILE, head_dim)) > 0.5
            keys = pick(k_ref, head, tile, part)
            src = final.at[head] if part == 1 else final_in.at[part // 2, head]
            scale = jnp.exp2(stat[head, part, 0, at, :] - src[0, at, :]) * src[1, at, :]
            attend = expo_ref[part, tile] * scale
            grad_scores = (attend * (gatt_ref[part, tile] - src[2, at, :])).astype(jnp.bfloat16)
            attend_b = attend.astype(jnp.bfloat16)
            dq = lax.dot_general(grad_scores, keys, TN, preferred_element_type=jnp.float32)
            rows_at = pl.ds(pl.multiple_of(tile * TILE, TILE), TILE)
            if part == 1:
                dq_own[rows_at, :] = dq * inv_root
            else:
                dq_side[part // 2, head, rows_at, :] = (dq * inv_root).astype(jnp.bfloat16)
            dk = jnp.dot(
                grad_scores, query_of(head, tile, part), preferred_element_type=jnp.float32
            )
            dv = jnp.dot(
                attend_b, grad_of(head, tile, part), preferred_element_type=jnp.float32
            )
            for which, term in ((0, dk), (1, dv)):
                for r in range(GH):
                    near = term[r * span : r * span + TILE]
                    far = term[r * span + TILE : (r + 1) * span]
                    adds = (
                        jnp.where(shifted, 0.0, near),
                        jnp.where(shifted, near, far),
                        jnp.where(shifted, far, 0.0),
                    )
                    for col, add in enumerate(adds):
                        where = pl.ds(
                            pl.multiple_of((r * GW + base + col) * TILE, TILE), TILE
                        )
                        acc[which, where, :] += add
            return carry

        lax.fori_loop(0, TPS, one, 0)

    def send_home(head):
        def stage(other, carry):
            at = pl.ds(pl.multiple_of(other * block, block), block)
            kv_out[head, other, 0] = (acc[0, at, :] * inv_root).astype(jnp.bfloat16)
            kv_out[head, other, 1] = acc[1, at, :].astype(jnp.bfloat16)
            return carry

        lax.fori_loop(0, rows, stage, 0)

        def one(step, carry):
            other = peer(step)
            pltpu.make_async_remote_copy(
                src_ref=kv_out.at[head, other],
                dst_ref=okv_ref.at[row * heads + head],
                send_sem=kv_send.at[head],
                recv_sem=kv_recv.at[head],
                device_id=(slab, other),
                device_id_type=MESH,
            ).start()
            return carry

        lax.fori_loop(1, rows, one, 0)
        okv_ref[row * heads + head] = kv_out[head, row]

    def send_dq(head):
        for n in range(2):
            to_side(
                dq_side.at[n, head], dq_in.at[1 - n, head], n, dq_send, dq_recv, head
            ).start()

    def finish_dq(head):
        for n in range(2):
            from_side(dq_in.at[n, head], n, dq_recv, head)

        def stage(other, carry):
            at = pl.ds(pl.multiple_of(other * block, block), block)
            total = (
                dq_mid[head][at, :]
                + dq_in[0, head, at, :].astype(jnp.float32)
                + dq_in[1, head, at, :].astype(jnp.float32)
            )
            dq_out[head, other] = total.astype(jnp.bfloat16)
            return carry

        lax.fori_loop(0, rows, stage, 0)

        def one(step, carry):
            other = peer(step)
            pltpu.make_async_remote_copy(
                src_ref=dq_out.at[head, other],
                dst_ref=oq_ref.at[row * heads + head],
                send_sem=o_send.at[head],
                recv_sem=o_recv.at[head],
                device_id=(slab, other),
                device_id_type=MESH,
            ).start()
            return carry

        lax.fori_loop(1, rows, one, 0)
        oq_ref[row * heads + head] = dq_out[head, row]

    dq_all = dq_own
    dq_mid = [dq_all.at[head] for head in range(heads)]

    send_queries(0)
    spread_grad(0)
    for head in range(heads):
        await_spread(g_own.at[head], a_send, a_recv, head)
        send_grads(head)
        if head + 1 < heads:
            spread_grad(head + 1)
            send_queries(head + 1)

    for head in range(heads):
        dq_own = dq_mid[head]
        acc[...] = jnp.zeros_like(acc)
        first_pass(head, 1)
        for n in range(2):
            from_side(q_side.at[n, head], n, q_recv, head)
            from_side(g_side.at[n, head], n, g_recv, head)
            first_pass(head, 2 * n)
        send_stats(head)
        combine(head)
        second_pass(head, 1)
        for n in range(2):
            from_side(final_in.at[n, head], n, f_recv, head)
            second_pass(head, 2 * n)
        send_dq(head)
        send_home(head)
    for head in range(heads):
        finish_dq(head)

    for head in range(heads):
        for n in range(2):
            to_side(q_ref.at[head], q_side.at[1 - n, head], n, q_send, q_recv, head).wait_send()
            to_side(g_own.at[head], g_side.at[1 - n, head], n, g_send, g_recv, head).wait_send()
            to_side(stat.at[head, 2 * n], stat_in.at[1 - n, head], n, s_send, s_recv, head).wait_send()
            to_side(final.at[head], final_in.at[1 - n, head], n, f_send, f_recv, head).wait_send()
            to_side(dq_side.at[n, head], dq_in.at[1 - n, head], n, dq_send, dq_recv, head).wait_send()
        await_spread(kv_out.at[head], kv_send, kv_recv, head)
    for head in range(heads):
        await_spread(dq_out.at[head], o_send, o_recv, head)


def fused_call(shift, bias, query, key, value, grad, slabs, rows):
    heads, tok_slab, head_dim = query.shape
    block = grad.shape[1]
    vmem = pl.BlockSpec(memory_space=pltpu.VMEM)
    keys_seen = GH * WIN_COLS * TILE
    pairs = heads * tok_slab * 3 * keys_seen
    low, full = jnp.bfloat16, jnp.float32
    side = pltpu.VMEM((2, heads, tok_slab, head_dim), low)
    return pl.pallas_call(
        functools.partial(fused_kernel, slabs, rows, head_dim ** (-0.5)),
        out_shape=(
            jax.ShapeDtypeStruct((rows * heads, block, head_dim), low),
            jax.ShapeDtypeStruct((rows * heads, 2, block, head_dim), low),
        ),
        in_specs=[vmem] * 6,
        out_specs=(vmem, vmem),
        scratch_shapes=[
            side,
            pltpu.VMEM((heads, rows, block, head_dim), low),
            pltpu.VMEM((2, heads, rows, block, head_dim), low),
            pltpu.VMEM((3, TPS, keys_seen, TILE), full),
            pltpu.VMEM((3, TPS, keys_seen, TILE), full),
            pltpu.VMEM((heads, 3, 3, TPS, TILE), full),
            pltpu.VMEM((2, heads, 3, TPS, TILE), full),
            pltpu.VMEM((heads, 3, TPS, TILE), full),
            pltpu.VMEM((2, heads, 3, TPS, TILE), full),
            pltpu.VMEM((2, tok_slab, head_dim), full),
            pltpu.VMEM((heads, rows, 2, block, head_dim), low),
            pltpu.VMEM((heads, tok_slab, head_dim), full),
            side,
            side,
            pltpu.VMEM((heads, rows, block, head_dim), low),
        ]
        + [
            pltpu.SemaphoreType.DMA((heads, 2)), pltpu.SemaphoreType.DMA((heads, 2)),
            pltpu.SemaphoreType.DMA((heads,)), pltpu.SemaphoreType.DMA((heads,)),
            pltpu.SemaphoreType.DMA((heads, 2)), pltpu.SemaphoreType.DMA((heads, 2)),
            pltpu.SemaphoreType.DMA((heads, 2)), pltpu.SemaphoreType.DMA((heads, 2)),
            pltpu.SemaphoreType.DMA((heads, 2)), pltpu.SemaphoreType.DMA((heads, 2)),
            pltpu.SemaphoreType.DMA((heads,)), pltpu.SemaphoreType.DMA((heads,)),
            pltpu.SemaphoreType.DMA((heads, 2)), pltpu.SemaphoreType.DMA((heads, 2)),
            pltpu.SemaphoreType.DMA((heads,)), pltpu.SemaphoreType.DMA((heads,)),
        ],
        compiler_params=pltpu.CompilerParams(
            collective_id=0, has_side_effects=True, vmem_limit_bytes=50 * 2**20
        ),
        cost_estimate=pl.CostEstimate(
            flops=10 * pairs * head_dim, bytes_accessed=8 * 2**20, transcendentals=pairs
        ),
    )(shift, bias, query, key, value, grad)


def window_terms(slabs, col_start, valid_tiles):
    slab = lax.axis_index("slab")
    tile = jnp.arange(TPS, dtype=jnp.int32)
    owners = slab + jnp.arange(-1, 2, dtype=jnp.int32)
    inside = (owners >= 0) & (owners < slabs)
    padded = jnp.pad(col_start.reshape(slabs, TPS), ((1, 1), (0, 0)))
    first = lax.dynamic_slice_in_dim(padded, slab, 3, 0)
    shift = first - (tile % GW) // 2
    slot = jnp.arange(GH * WIN_COLS, dtype=jnp.int32)
    inner = (slot // WIN_COLS * GW + slot % WIN_COLS)[:, None, None] + first
    limit = lax.dynamic_index_in_dim(valid_tiles, slab, 0, False)
    bias = jnp.where((inner < limit) & inside[:, None], 0.0, NEG)
    wide = lambda a: jnp.broadcast_to(a.astype(jnp.float32)[..., None], a.shape + (TILE,))
    return wide(shift), wide(bias)


def on_device(slabs, rows, queries, keys, values, out_grad, col_start, valid_tiles):
    shift, bias = window_terms(slabs, col_start, valid_tiles)
    dq, dkv = fused_call(
        shift, bias, queries.swapaxes(0, 1), keys.swapaxes(0, 1),
        values.swapaxes(0, 1), out_grad.swapaxes(0, 1), slabs, rows,
    )
    return dq.swapaxes(0, 1), dkv[:, 0].swapaxes(0, 1), dkv[:, 1].swapaxes(0, 1)


def solution(mesh):
    head_split = P("slab", "row", None)
    token_split = P(("slab", "row"), None, None)
    return jax.shard_map(
        functools.partial(on_device, mesh.shape["slab"], mesh.shape["row"]),
        mesh=mesh,
        in_specs=(head_split, head_split, head_split, token_split, P(), P()),
        out_specs=(token_split,) * 3,
        check_vma=False,
    )
```

```python
import functools

import jax
import jax.numpy as jnp
from jax import lax
from jax.experimental import pallas as pl
from jax.experimental.pallas import tpu as pltpu
from jax.sharding import PartitionSpec as P

TILE = 128
GH = 2
GW = 4
WIN_COLS = 2
TPS = 8
RUN = 8
NEG = -1e30
LOG2E = 1.4426950408889634
MESH = pl.DeviceIdType.MESH
NT = (((1,), (1,)), ((), ()))
TN = (((0,), (0,)), ((), ()))


def fused_kernel(
    slabs, rows, inv_root, shift_ref, bias_ref, q_ref, k_ref, v_ref, g_ref,
    oq_ref, okv_ref,
    q_side, g_own, g_side, expo_ref, gatt_ref, stat, stat_in, final, final_in,
    acc, kv_out, dq_own, dq_side, dq_in, dq_out,
    q_send, q_recv, a_send, a_recv, g_send, g_recv, s_send, s_recv, f_send, f_recv,
    kv_send, kv_recv, dq_send, dq_recv, o_send, o_recv,
):
    heads, tok_slab, head_dim = q_ref.shape
    block = g_ref.shape[1]
    span = WIN_COLS * TILE
    row_len = GW * TILE
    slab = lax.axis_index("slab")
    row = lax.axis_index("row")
    below = lax.rem(slab + slabs - 1, slabs)
    above = lax.rem(slab + 1, slabs)
    sides = (below, above)
    half = rows // 2
    group = row // half
    mine, others = group * half, (1 - group) * half
    edges = (slab % RUN == 0, slab % RUN == RUN - 1)

    def peer(step):
        return lax.rem(row + step, rows)

    barrier = pltpu.get_barrier_semaphore()
    for side in sides:
        pl.semaphore_signal(barrier, inc=1, device_id=(side, row), device_id_type=MESH)

    def greet(step, carry):
        pl.semaphore_signal(barrier, inc=1, device_id=(slab, peer(step)), device_id_type=MESH)
        return carry

    lax.fori_loop(1, rows, greet, 0)
    for n in range(2):

        @pl.when(edges[n])
        def _():
            def greet_far(step, carry):
                pl.semaphore_signal(
                    barrier, inc=1, device_id=(sides[n], others + step), device_id_type=MESH
                )
                return carry

            lax.fori_loop(0, half, greet_far, 0)

    at_edge = jnp.logical_or(edges[0], edges[1])
    pl.semaphore_wait(barrier, rows + 1 + jnp.where(at_edge, half, 0))


    def to_side(src, dst, n, send, recv, head):
        return pltpu.make_async_remote_copy(
            src_ref=src,
            dst_ref=dst,
            send_sem=send.at[head, n],
            recv_sem=recv.at[head, 1 - n],
            device_id=(sides[n], row),
            device_id_type=MESH,
        )

    def from_side(ref, n, recv, head):
        pltpu.make_async_copy(ref, ref, recv.at[head, n]).wait()

    def all_sent(ref, sem):
        pltpu.make_async_copy(ref, ref, sem).wait()

    def send_queries(head):
        for n in range(2):
            to_side(q_ref.at[head], q_side.at[1 - n, head], n, q_send, q_recv, head).start()

    def spread_grad(head):
        def one(step, carry):
            other = peer(step)
            pltpu.make_async_remote_copy(
                src_ref=g_ref.at[other * heads + head],
                dst_ref=g_own.at[head, row],
                send_sem=a_send.at[head],
                recv_sem=a_recv.at[head],
                device_id=(slab, other),
                device_id_type=MESH,
            ).start()
            return carry

        lax.fori_loop(1, rows, one, 0)
        g_own[head, row] = g_ref[row * heads + head]

    def await_spread(buffer, send, recv, head):
        whole = buffer.at[pl.ds(0, rows - 1)]
        pltpu.make_async_copy(whole, whole, recv.at[head]).wait()
        pltpu.make_async_copy(whole, whole, send.at[head]).wait()

    def blocks_to_side(own, far, inbox, n, send, recv, head):
        @pl.when(jnp.logical_not(edges[n]))
        def _():
            to_side(own, inbox.at[1 - n, head], n, send, recv, head).start()

        @pl.when(edges[n])
        def _():
            near = pl.ds(mine, half)
            to_side(own.at[near], inbox.at[1 - n, head, near], n, send, recv, head).start()
            if far is not None:
                far(n, head)

    def far_copies(block_of, inbox, n, send, recv, head):
        def one(step, carry):
            other = others + step
            pltpu.make_async_remote_copy(
                src_ref=block_of(other),
                dst_ref=inbox.at[1 - n, head, row],
                send_sem=send.at[head, n],
                recv_sem=recv.at[head, 1 - n],
                device_id=(sides[n], other),
                device_id_type=MESH,
            ).start()
            return carry

        lax.fori_loop(0, half, one, 0)

    def spread_far(head):
        for n in range(2):

            @pl.when(edges[n])
            def _():
                far_copies(
                    lambda other: g_ref.at[other * heads + head], g_side, n, g_send, g_recv, head
                )

    def send_grads(head):
        for n in range(2):
            blocks_to_side(g_own.at[head], None, g_side, n, g_send, g_recv, head)

    def pick(ref, head, tile, part):
        base = (tile % GW) // 2
        high = jnp.broadcast_to(shift_ref[part, pl.ds(tile, 1), :], (TILE, head_dim))
        high = high.astype(jnp.bfloat16)
        low = 1 - high
        chosen = []
        for r in range(GH):
            cols = [
                ref[head, pl.ds(pl.multiple_of((r * GW + base + c) * TILE, TILE), TILE), :]
                for c in range(WIN_COLS + 1)
            ]
            chosen += [cols[c] * low + cols[c + 1] * high for c in range(WIN_COLS)]
        return jnp.concatenate(chosen, axis=0)

    def query_of(head, tile, part):
        at = pl.ds(pl.multiple_of(tile * TILE, TILE), TILE)
        if part == 1:
            return q_ref[head, at, :]
        return q_side[part // 2, head, at, :]

    def grad_of(head, tile, part):
        each = TILE // block
        at = pl.ds(tile * each, each)
        if part == 1:
            return g_own[head, at].reshape(TILE, head_dim)
        return g_side[part // 2, head, at].reshape(TILE, head_dim)

    def first_pass(head, part):
        def one(tile, carry):
            keys = pick(k_ref, head, tile, part)
            values = pick(v_ref, head, tile, part)
            bias = jnp.concatenate(
                [
                    jnp.broadcast_to(bias_ref[n, part, pl.ds(tile, 1), :], (TILE, TILE))
                    for n in range(GH * WIN_COLS)
                ],
                axis=0,
            )
            scores = lax.dot_general(
                keys, query_of(head, tile, part), NT, preferred_element_type=jnp.float32
            )
            scores = scores * (inv_root * LOG2E) + bias
            peak = jnp.max(scores, axis=0, keepdims=True)
            expo = jnp.exp2(scores - peak)
            grad_attend = lax.dot_general(
                values, grad_of(head, tile, part), NT, preferred_element_type=jnp.float32
            )
            expo_ref[head, part, tile] = expo
            gatt_ref[head, part, tile] = grad_attend
            at = pl.ds(tile, 1)
            stat[head, part, 0, at, :] = peak
            stat[head, part, 1, at, :] = jnp.sum(expo, axis=0, keepdims=True)
            stat[head, part, 2, at, :] = jnp.sum(expo * grad_attend, axis=0, keepdims=True)
            return carry

        lax.fori_loop(0, TPS, one, 0)

    def send_stats(head):
        for n in range(2):
            to_side(
                stat.at[head, 2 * n], stat_in.at[1 - n, head], n, s_send, s_recv, head
            ).start()

    def combine(head):
        for n in range(2):
            from_side(stat_in.at[n, head], n, s_recv, head)
        peaks = [stat_in[0, head, 0], stat[head, 1, 0], stat_in[1, head, 0]]
        sums = [stat_in[0, head, 1], stat[head, 1, 1], stat_in[1, head, 1]]
        dots = [stat_in[0, head, 2], stat[head, 1, 2], stat_in[1, head, 2]]
        top = jnp.maximum(jnp.maximum(peaks[0], peaks[1]), peaks[2])
        weights = [jnp.exp2(p - top) for p in peaks]
        total = sum(w * s for w, s in zip(weights, sums))
        final[head, 0] = top
        final[head, 1] = 1.0 / total
        final[head, 2] = sum(w * d for w, d in zip(weights, dots)) / total
        for n in range(2):
            to_side(
                final.at[head], final_in.at[1 - n, head], n, f_send, f_recv, head
            ).start()

    def second_pass(head, part):
        def one(tile, carry):
            base = (tile % GW) // 2
            at = pl.ds(tile, 1)
            shifted = jnp.broadcast_to(shift_ref[part, at, :], (TILE, head_dim)) > 0.5
            keys = pick(k_ref, head, tile, part)
            src = final.at[head] if part == 1 else final_in.at[part // 2, head]
            scale = jnp.exp2(stat[head, part, 0, at, :] - src[0, at, :]) * src[1, at, :]
            attend = expo_ref[head, part, tile] * scale
            grad_scores = (attend * (gatt_ref[head, part, tile] - src[2, at, :])).astype(jnp.bfloat16)
            attend_b = attend.astype(jnp.bfloat16)
            dq = lax.dot_general(grad_scores, keys, TN, preferred_element_type=jnp.float32)
            rows_at = pl.ds(pl.multiple_of(tile * TILE, TILE), TILE)
            if part == 1:
                dq_own[head, rows_at, :] = dq * inv_root
            else:
                each = TILE // block
                dq_side[part // 2, head, pl.ds(tile * each, each)] = (
                    (dq * inv_root).astype(jnp.bfloat16).reshape(each, block, head_dim)
                )
            dk = jnp.dot(
                grad_scores, query_of(head, tile, part), preferred_element_type=jnp.float32
            )
            dv = jnp.dot(
                attend_b, grad_of(head, tile, part), preferred_element_type=jnp.float32
            )
            for which, term in ((0, dk), (1, dv)):
                for r in range(GH):
                    near = term[r * span : r * span + TILE]
                    far = term[r * span + TILE : (r + 1) * span]
                    adds = (
                        jnp.where(shifted, 0.0, near),
                        jnp.where(shifted, near, far),
                        jnp.where(shifted, far, 0.0),
                    )
                    for col, add in enumerate(adds):
                        where = pl.ds(
                            pl.multiple_of((r * GW + base + col) * TILE, TILE), TILE
                        )
                        acc[which, where, :] += add
            return carry

        lax.fori_loop(0, TPS, one, 0)

    def send_home(head):
        def stage(other, carry):
            at = pl.ds(pl.multiple_of(other * block, block), block)
            kv_out[head, other, 0] = (acc[0, at, :] * inv_root).astype(jnp.bfloat16)
            kv_out[head, other, 1] = acc[1, at, :].astype(jnp.bfloat16)
            return carry

        lax.fori_loop(0, rows, stage, 0)

        def one(step, carry):
            other = peer(step)
            pltpu.make_async_remote_copy(
                src_ref=kv_out.at[head, other],
                dst_ref=okv_ref.at[row * heads + head],
                send_sem=kv_send.at[head],
                recv_sem=kv_recv.at[head],
                device_id=(slab, other),
                device_id_type=MESH,
            ).start()
            return carry

        lax.fori_loop(1, rows, one, 0)
        okv_ref[row * heads + head] = kv_out[head, row]

    def send_dq(head, n):
        def far(n, head):
            far_copies(
                lambda other: dq_side.at[n, head, other], dq_in, n, dq_send, dq_recv, head
            )

        blocks_to_side(dq_side.at[n, head], far, dq_in, n, dq_send, dq_recv, head)

    def finish_dq(head):
        for n in range(2):
            from_side(dq_in.at[n, head], n, dq_recv, head)

        def stage(other, carry):
            at = pl.ds(pl.multiple_of(other * block, block), block)
            total = dq_own[head, at, :]
            for n in range(2):
                here = jnp.logical_or(jnp.logical_not(edges[n]), other // half == group)
                total += jnp.where(here, dq_in[n, head, other].astype(jnp.float32), 0.0)
            dq_out[head, other] = total.astype(jnp.bfloat16)
            return carry

        lax.fori_loop(0, rows, stage, 0)

        def one(step, carry):
            other = peer(step)
            pltpu.make_async_remote_copy(
                src_ref=dq_out.at[head, other],
                dst_ref=oq_ref.at[row * heads + head],
                send_sem=o_send.at[head],
                recv_sem=o_recv.at[head],
                device_id=(slab, other),
                device_id_type=MESH,
            ).start()
            return carry

        lax.fori_loop(1, rows, one, 0)
        oq_ref[row * heads + head] = dq_out[head, row]

    def sides_pass(head):
        for n in range(2):
            from_side(q_side.at[n, head], n, q_recv, head)
            from_side(g_side.at[n, head], n, g_recv, head)
            first_pass(head, 2 * n)
        send_stats(head)

    def results(head):
        acc[...] = jnp.zeros_like(acc)
        for n in range(2):
            from_side(final_in.at[n, head], n, f_recv, head)
            second_pass(head, 2 * n)
            send_dq(head, n)
        second_pass(head, 1)
        send_home(head)

    for head in range(heads):
        spread_far(head)
        spread_grad(head)
    for head in range(heads):
        send_queries(head)
    await_spread(g_own.at[0], a_send, a_recv, 0)
    send_grads(0)
    first_pass(0, 1)
    await_spread(g_own.at[1], a_send, a_recv, 1)
    send_grads(1)
    sides_pass(0)
    first_pass(1, 1)
    combine(0)
    sides_pass(1)
    results(0)
    combine(1)
    results(1)
    for head in range(heads):
        finish_dq(head)

    for head in range(heads):
        for n in range(2):
            to_side(q_ref.at[head], q_side.at[1 - n, head], n, q_send, q_recv, head).wait_send()
            to_side(g_own.at[head], g_side.at[1 - n, head], n, g_send, g_recv, head).wait_send()
            to_side(stat.at[head, 2 * n], stat_in.at[1 - n, head], n, s_send, s_recv, head).wait_send()
            to_side(final.at[head], final_in.at[1 - n, head], n, f_send, f_recv, head).wait_send()
            to_side(dq_side.at[n, head], dq_in.at[1 - n, head], n, dq_send, dq_recv, head).wait_send()
        await_spread(kv_out.at[head], kv_send, kv_recv, head)
    for head in range(heads):
        await_spread(dq_out.at[head], o_send, o_recv, head)
        for n in range(2):

            @pl.when(edges[n])
            def _():
                def add(step, carry):
                    other = others + step
                    at = other * heads + head
                    total = oq_ref[at].astype(jnp.float32) + dq_in[n, head, other].astype(jnp.float32)
                    oq_ref[at] = total.astype(jnp.bfloat16)
                    return carry

                lax.fori_loop(0, half, add, 0)


def fused_call(shift, bias, query, key, value, grad, slabs, rows):
    heads, tok_slab, head_dim = query.shape
    block = grad.shape[1]
    vmem = pl.BlockSpec(memory_space=pltpu.VMEM)
    keys_seen = GH * WIN_COLS * TILE
    pairs = heads * tok_slab * 3 * keys_seen
    low, full = jnp.bfloat16, jnp.float32
    side = pltpu.VMEM((2, heads, tok_slab, head_dim), low)
    blocks = pltpu.VMEM((2, heads, rows, block, head_dim), low)
    return pl.pallas_call(
        functools.partial(fused_kernel, slabs, rows, head_dim ** (-0.5)),
        out_shape=(
            jax.ShapeDtypeStruct((rows * heads, block, head_dim), low),
            jax.ShapeDtypeStruct((rows * heads, 2, block, head_dim), low),
        ),
        in_specs=[vmem] * 6,
        out_specs=(vmem, vmem),
        scratch_shapes=[
            side,
            pltpu.VMEM((heads, rows, block, head_dim), low),
            blocks,
            pltpu.VMEM((heads, 3, TPS, keys_seen, TILE), full),
            pltpu.VMEM((heads, 3, TPS, keys_seen, TILE), full),
            pltpu.VMEM((heads, 3, 3, TPS, TILE), full),
            pltpu.VMEM((2, heads, 3, TPS, TILE), full),
            pltpu.VMEM((heads, 3, TPS, TILE), full),
            pltpu.VMEM((2, heads, 3, TPS, TILE), full),
            pltpu.VMEM((2, tok_slab, head_dim), full),
            pltpu.VMEM((heads, rows, 2, block, head_dim), low),
            pltpu.VMEM((heads, tok_slab, head_dim), full),
            blocks,
            blocks,
            pltpu.VMEM((heads, rows, block, head_dim), low),
        ]
        + [
            pltpu.SemaphoreType.DMA((heads, 2)), pltpu.SemaphoreType.DMA((heads, 2)),
            pltpu.SemaphoreType.DMA((heads,)), pltpu.SemaphoreType.DMA((heads,)),
            pltpu.SemaphoreType.DMA((heads, 2)), pltpu.SemaphoreType.DMA((heads, 2)),
            pltpu.SemaphoreType.DMA((heads, 2)), pltpu.SemaphoreType.DMA((heads, 2)),
            pltpu.SemaphoreType.DMA((heads, 2)), pltpu.SemaphoreType.DMA((heads, 2)),
            pltpu.SemaphoreType.DMA((heads,)), pltpu.SemaphoreType.DMA((heads,)),
            pltpu.SemaphoreType.DMA((heads, 2)), pltpu.SemaphoreType.DMA((heads, 2)),
            pltpu.SemaphoreType.DMA((heads,)), pltpu.SemaphoreType.DMA((heads,)),
        ],
        compiler_params=pltpu.CompilerParams(
            collective_id=0, has_side_effects=True, vmem_limit_bytes=50 * 2**20
        ),
        cost_estimate=pl.CostEstimate(
            flops=10 * pairs * head_dim, bytes_accessed=8 * 2**20, transcendentals=pairs
        ),
    )(shift, bias, query, key, value, grad)


def window_terms(slabs, col_start, valid_tiles):
    slab = lax.axis_index("slab")
    tile = jnp.arange(TPS, dtype=jnp.int32)
    owners = slab + jnp.arange(-1, 2, dtype=jnp.int32)
    inside = (owners >= 0) & (owners < slabs)
    padded = jnp.pad(col_start.reshape(slabs, TPS), ((1, 1), (0, 0)))
    first = lax.dynamic_slice_in_dim(padded, slab, 3, 0)
    shift = first - (tile % GW) // 2
    slot = jnp.arange(GH * WIN_COLS, dtype=jnp.int32)
    inner = (slot // WIN_COLS * GW + slot % WIN_COLS)[:, None, None] + first
    limit = lax.dynamic_index_in_dim(valid_tiles, slab, 0, False)
    bias = jnp.where((inner < limit) & inside[:, None], 0.0, NEG)
    wide = lambda a: jnp.broadcast_to(a.astype(jnp.float32)[..., None], a.shape + (TILE,))
    return wide(shift), wide(bias)


def on_device(slabs, rows, queries, keys, values, out_grad, col_start, valid_tiles):
    shift, bias = window_terms(slabs, col_start, valid_tiles)
    dq, dkv = fused_call(
        shift, bias, queries.swapaxes(0, 1), keys.swapaxes(0, 1),
        values.swapaxes(0, 1), out_grad.swapaxes(0, 1), slabs, rows,
    )
    return dq.swapaxes(0, 1), dkv[:, 0].swapaxes(0, 1), dkv[:, 1].swapaxes(0, 1)


def solution(mesh):
    head_split = P("slab", "row", None)
    token_split = P(("slab", "row"), None, None)
    return jax.shard_map(
        functools.partial(on_device, mesh.shape["slab"], mesh.shape["row"]),
        mesh=mesh,
        in_specs=(head_split, head_split, head_split, token_split, P(), P()),
        out_specs=(token_split,) * 3,
        check_vma=False,
    )
```

```python
import functools

import jax
import jax.numpy as jnp
from jax import lax
from jax.experimental import pallas as pl
from jax.experimental.pallas import tpu as pltpu
from jax.sharding import PartitionSpec as P

TILE = 128
GH = 2
GW = 4
WIN_COLS = 2
TPS = 8
RUN = 8
NEG = -1e30
LOG2E = 1.4426950408889634
MESH = pl.DeviceIdType.MESH
NT = (((1,), (1,)), ((), ()))
TN = (((0,), (0,)), ((), ()))


def fused_kernel(
    slabs, rows, inv_root, cols_ref, counts_ref, q_ref, k_ref, v_ref, g_ref,
    oq_ref, okv_ref,
    q_side, g_own, g_side, expo_ref, gatt_ref, peaks, stat, stat_in, final,
    acc, kv_out, dq_own, dq_side, dq_in, dq_out,
    q_send, q_recv, a_send, a_recv, g_send, g_recv, s_send, s_recv,
    kv_send, kv_recv, dq_send, dq_recv, o_send, o_recv,
):
    heads, tok_slab, head_dim = q_ref.shape
    block = g_ref.shape[1]
    span = WIN_COLS * TILE
    row_len = GW * TILE
    slab = lax.axis_index("slab")
    row = lax.axis_index("row")
    below = lax.rem(slab + slabs - 1, slabs)
    above = lax.rem(slab + 1, slabs)
    sides = (below, above)
    half = rows // 2
    group = row // half
    mine, others = group * half, (1 - group) * half
    edges = (slab % RUN == 0, slab % RUN == RUN - 1)

    def peer(step):
        return lax.rem(row + step, rows)

    barrier = pltpu.get_barrier_semaphore()
    two_below = lax.rem(slab + slabs - 2, slabs)
    two_above = lax.rem(slab + 2, slabs)
    for side in (two_below, below, above, two_above):
        pl.semaphore_signal(barrier, inc=1, device_id=(side, row), device_id_type=MESH)

    def greet(step, carry):
        pl.semaphore_signal(barrier, inc=1, device_id=(slab, peer(step)), device_id_type=MESH)
        return carry

    lax.fori_loop(1, rows, greet, 0)
    for n in range(2):

        @pl.when(edges[n])
        def _():
            def greet_far(step, carry):
                pl.semaphore_signal(
                    barrier, inc=1, device_id=(sides[n], others + step), device_id_type=MESH
                )
                return carry

            lax.fori_loop(0, half, greet_far, 0)

    at_edge = jnp.logical_or(edges[0], edges[1])
    pl.semaphore_wait(barrier, rows + 3 + jnp.where(at_edge, half, 0))


    def to_side(src, dst, n, send, recv, head):
        return pltpu.make_async_remote_copy(
            src_ref=src,
            dst_ref=dst,
            send_sem=send.at[head, n],
            recv_sem=recv.at[head, 1 - n],
            device_id=(sides[n], row),
            device_id_type=MESH,
        )

    def from_side(ref, n, recv, head):
        pltpu.make_async_copy(ref, ref, recv.at[head, n]).wait()

    def all_sent(ref, sem):
        pltpu.make_async_copy(ref, ref, sem).wait()

    def send_queries(head):
        for n in range(2):
            to_side(q_ref.at[head], q_side.at[1 - n, head], n, q_send, q_recv, head).start()

    def spread_grad(head):
        def one(step, carry):
            other = peer(step)
            pltpu.make_async_remote_copy(
                src_ref=g_ref.at[other * heads + head],
                dst_ref=g_own.at[head, row],
                send_sem=a_send.at[head],
                recv_sem=a_recv.at[head],
                device_id=(slab, other),
                device_id_type=MESH,
            ).start()
            return carry

        lax.fori_loop(1, rows, one, 0)
        g_own[head, row] = g_ref[row * heads + head]

    def await_spread(buffer, send, recv, head):
        whole = buffer.at[pl.ds(0, rows - 1)]
        pltpu.make_async_copy(whole, whole, recv.at[head]).wait()
        pltpu.make_async_copy(whole, whole, send.at[head]).wait()

    def blocks_to_side(own, far, inbox, n, send, recv, head):
        @pl.when(jnp.logical_not(edges[n]))
        def _():
            to_side(own, inbox.at[1 - n, head], n, send, recv, head).start()

        @pl.when(edges[n])
        def _():
            near = pl.ds(mine, half)
            to_side(own.at[near], inbox.at[1 - n, head, near], n, send, recv, head).start()
            if far is not None:
                far(n, head)

    def far_copies(block_of, inbox, n, send, recv, head):
        def one(step, carry):
            other = others + step
            pltpu.make_async_remote_copy(
                src_ref=block_of(other),
                dst_ref=inbox.at[1 - n, head, row],
                send_sem=send.at[head, n],
                recv_sem=recv.at[head, 1 - n],
                device_id=(sides[n], other),
                device_id_type=MESH,
            ).start()
            return carry

        lax.fori_loop(0, half, one, 0)

    def spread_far(head):
        for n in range(2):

            @pl.when(edges[n])
            def _():
                far_copies(
                    lambda other: g_ref.at[other * heads + head], g_side, n, g_send, g_recv, head
                )

    def send_grads(head):
        for n in range(2):
            blocks_to_side(g_own.at[head], None, g_side, n, g_send, g_recv, head)

    def first_of(tile, part):
        owner = (below, slab, above)[part]
        return jnp.full((1, TILE), cols_ref[owner * TPS + tile], jnp.int32)

    def shift_of(tile, part):
        return (first_of(tile, part) - (tile % GW) // 2).astype(jnp.float32)

    limit = jnp.full((1, TILE), counts_ref[slab], jnp.int32)
    inside = (slab > 0, None, slab < slabs - 1)

    def bias_of(slot, tile, part):
        reach = limit if part == 1 else jnp.where(inside[part], limit, 0)
        inner = first_of(tile, part) + (slot // WIN_COLS * GW + slot % WIN_COLS)
        return jnp.where(inner < reach, 0.0, NEG)

    def pick(ref, head, tile, part):
        base = (tile % GW) // 2
        high = jnp.broadcast_to(shift_of(tile, part), (TILE, head_dim)).astype(jnp.bfloat16)
        low = 1 - high
        chosen = []
        for r in range(GH):
            cols = [
                ref[head, pl.ds(pl.multiple_of((r * GW + base + c) * TILE, TILE), TILE), :]
                for c in range(WIN_COLS + 1)
            ]
            chosen += [cols[c] * low + cols[c + 1] * high for c in range(WIN_COLS)]
        return jnp.concatenate(chosen, axis=0)

    def query_of(head, tile, part):
        at = pl.ds(pl.multiple_of(tile * TILE, TILE), TILE)
        if part == 1:
            return q_ref[head, at, :]
        return q_side[part // 2, head, at, :]

    def grad_of(head, tile, part):
        each = TILE // block
        at = pl.ds(tile * each, each)
        if part == 1:
            return g_own[head, at].reshape(TILE, head_dim)
        return g_side[part // 2, head, at].reshape(TILE, head_dim)

    def first_pass(head, part):
        def one(tile, carry):
            keys = pick(k_ref, head, tile, part)
            values = pick(v_ref, head, tile, part)
            bias = jnp.concatenate(
                [
                    jnp.broadcast_to(bias_of(n, tile, part), (TILE, TILE))
                    for n in range(GH * WIN_COLS)
                ],
                axis=0,
            )
            scores = lax.dot_general(
                keys, query_of(head, tile, part), NT, preferred_element_type=jnp.float32
            )
            scores = scores * (inv_root * LOG2E) + bias
            peak = jnp.max(scores, axis=0, keepdims=True)
            expo = jnp.exp2(scores - peak)
            grad_attend = lax.dot_general(
                values, grad_of(head, tile, part), NT, preferred_element_type=jnp.float32
            )
            expo_ref[head, part, tile] = expo
            gatt_ref[head, part, tile] = grad_attend
            at = pl.ds(tile, 1)
            total = jnp.sum(expo, axis=0, keepdims=True)
            dot = jnp.sum(expo * grad_attend, axis=0, keepdims=True)
            peaks[head, part, at, :] = peak
            stat[head, part, 0, at, :] = peak + jnp.log2(total)
            stat[head, part, 1, at, :] = dot / total
            return carry

        lax.fori_loop(0, TPS, one, 0)

    routes = (
        (1, above, 0, 0), (2, two_above, 0, 1), (0, below, 1, 0),
        (2, above, 1, 1), (0, two_below, 2, 0), (1, below, 2, 1),
    )

    def stat_copy(head, route):
        part, target, there, slot = route
        return pltpu.make_async_remote_copy(
            src_ref=stat.at[head, part],
            dst_ref=stat_in.at[head, there, slot],
            send_sem=s_send.at[head, there, slot],
            recv_sem=s_recv.at[head, there, slot],
            device_id=(target, row),
            device_id_type=MESH,
        )

    def send_stats(head):
        for route in routes:
            stat_copy(head, route).start()

    def combine(head, part):
        for slot in range(2):
            ref = stat_in.at[head, part, slot]
            pltpu.make_async_copy(ref, ref, s_recv.at[head, part, slot]).wait()
        logs = [stat[head, part, 0], stat_in[head, part, 0, 0], stat_in[head, part, 1, 0]]
        dots = [stat[head, part, 1], stat_in[head, part, 0, 1], stat_in[head, part, 1, 1]]
        top = jnp.maximum(jnp.maximum(logs[0], logs[1]), logs[2])
        weights = [jnp.exp2(one - top) for one in logs]
        total = weights[0] + weights[1] + weights[2]
        final[head, part, 0] = jnp.exp2(peaks[head, part] - top) / total
        final[head, part, 1] = (
            weights[0] * dots[0] + weights[1] * dots[1] + weights[2] * dots[2]
        ) / total

    def second_pass(head, part):
        def one(tile, carry):
            base = (tile % GW) // 2
            at = pl.ds(tile, 1)
            shifted = jnp.broadcast_to(shift_of(tile, part), (TILE, head_dim)) > 0.5
            keys = pick(k_ref, head, tile, part)
            attend = expo_ref[head, part, tile] * final[head, part, 0, at, :]
            grad_scores = attend * (gatt_ref[head, part, tile] - final[head, part, 1, at, :])
            grad_scores = grad_scores.astype(jnp.bfloat16)
            attend_b = attend.astype(jnp.bfloat16)
            dq = lax.dot_general(grad_scores, keys, TN, preferred_element_type=jnp.float32)
            rows_at = pl.ds(pl.multiple_of(tile * TILE, TILE), TILE)
            if part == 1:
                dq_own[head, rows_at, :] = dq * inv_root
            else:
                each = TILE // block
                dq_side[part // 2, head, pl.ds(tile * each, each)] = (
                    (dq * inv_root).astype(jnp.bfloat16).reshape(each, block, head_dim)
                )
            dk = jnp.dot(
                grad_scores, query_of(head, tile, part), preferred_element_type=jnp.float32
            )
            dv = jnp.dot(
                attend_b, grad_of(head, tile, part), preferred_element_type=jnp.float32
            )
            for which, term in ((0, dk), (1, dv)):
                for r in range(GH):
                    near = term[r * span : r * span + TILE]
                    far = term[r * span + TILE : (r + 1) * span]
                    adds = (
                        jnp.where(shifted, 0.0, near),
                        jnp.where(shifted, near, far),
                        jnp.where(shifted, far, 0.0),
                    )
                    for col, add in enumerate(adds):
                        where = pl.ds(
                            pl.multiple_of((r * GW + base + col) * TILE, TILE), TILE
                        )
                        acc[which, where, :] += add
            return carry

        lax.fori_loop(0, TPS, one, 0)

    def send_home(head):
        def stage(other, carry):
            at = pl.ds(pl.multiple_of(other * block, block), block)
            kv_out[head, other, 0] = (acc[0, at, :] * inv_root).astype(jnp.bfloat16)
            kv_out[head, other, 1] = acc[1, at, :].astype(jnp.bfloat16)
            return carry

        lax.fori_loop(0, rows, stage, 0)

        def one(step, carry):
            other = peer(step)
            pltpu.make_async_remote_copy(
                src_ref=kv_out.at[head, other],
                dst_ref=okv_ref.at[row * heads + head],
                send_sem=kv_send.at[head],
                recv_sem=kv_recv.at[head],
                device_id=(slab, other),
                device_id_type=MESH,
            ).start()
            return carry

        lax.fori_loop(1, rows, one, 0)
        okv_ref[row * heads + head] = kv_out[head, row]

    def send_dq(head, n):
        def far(n, head):
            far_copies(
                lambda other: dq_side.at[n, head, other], dq_in, n, dq_send, dq_recv, head
            )

        blocks_to_side(dq_side.at[n, head], far, dq_in, n, dq_send, dq_recv, head)

    def finish_dq(head):
        for n in range(2):
            from_side(dq_in.at[n, head], n, dq_recv, head)

        def stage(other, carry):
            at = pl.ds(pl.multiple_of(other * block, block), block)
            total = dq_own[head, at, :]
            for n in range(2):
                here = jnp.logical_or(jnp.logical_not(edges[n]), other // half == group)
                total += jnp.where(here, dq_in[n, head, other].astype(jnp.float32), 0.0)
            dq_out[head, other] = total.astype(jnp.bfloat16)
            return carry

        lax.fori_loop(0, rows, stage, 0)

        def one(step, carry):
            other = peer(step)
            pltpu.make_async_remote_copy(
                src_ref=dq_out.at[head, other],
                dst_ref=oq_ref.at[row * heads + head],
                send_sem=o_send.at[head],
                recv_sem=o_recv.at[head],
                device_id=(slab, other),
                device_id_type=MESH,
            ).start()
            return carry

        lax.fori_loop(1, rows, one, 0)
        oq_ref[row * heads + head] = dq_out[head, row]

    def sides_pass(head):
        for n in range(2):
            from_side(q_side.at[n, head], n, q_recv, head)
            from_side(g_side.at[n, head], n, g_recv, head)
            first_pass(head, 2 * n)
        send_stats(head)

    def results(head):
        acc[...] = jnp.zeros_like(acc)
        for n in range(2):
            combine(head, 2 * n)
            second_pass(head, 2 * n)
            send_dq(head, n)
        combine(head, 1)
        second_pass(head, 1)
        send_home(head)

    for head in range(heads):
        spread_far(head)
        spread_grad(head)
    for head in range(heads):
        send_queries(head)
    await_spread(g_own.at[0], a_send, a_recv, 0)
    send_grads(0)
    first_pass(0, 1)
    await_spread(g_own.at[1], a_send, a_recv, 1)
    send_grads(1)
    sides_pass(0)
    first_pass(1, 1)
    sides_pass(1)
    results(0)
    results(1)
    for head in range(heads):
        finish_dq(head)

    for head in range(heads):
        for n in range(2):
            to_side(q_ref.at[head], q_side.at[1 - n, head], n, q_send, q_recv, head).wait_send()
            to_side(g_own.at[head], g_side.at[1 - n, head], n, g_send, g_recv, head).wait_send()
            to_side(dq_side.at[n, head], dq_in.at[1 - n, head], n, dq_send, dq_recv, head).wait_send()
        for route in routes:
            stat_copy(head, route).wait_send()
        await_spread(kv_out.at[head], kv_send, kv_recv, head)
    for head in range(heads):
        await_spread(dq_out.at[head], o_send, o_recv, head)
        for n in range(2):

            @pl.when(edges[n])
            def _():
                def add(step, carry):
                    other = others + step
                    at = other * heads + head
                    total = oq_ref[at].astype(jnp.float32) + dq_in[n, head, other].astype(jnp.float32)
                    oq_ref[at] = total.astype(jnp.bfloat16)
                    return carry

                lax.fori_loop(0, half, add, 0)


def fused_call(cols, counts, query, key, value, grad, slabs, rows):
    heads, tok_slab, head_dim = query.shape
    block = grad.shape[1]
    vmem = pl.BlockSpec(memory_space=pltpu.VMEM)
    smem = pl.BlockSpec(memory_space=pltpu.SMEM)
    keys_seen = GH * WIN_COLS * TILE
    pairs = heads * tok_slab * 3 * keys_seen
    low, full = jnp.bfloat16, jnp.float32
    side = pltpu.VMEM((2, heads, tok_slab, head_dim), low)
    blocks = pltpu.VMEM((2, heads, rows, block, head_dim), low)
    return pl.pallas_call(
        functools.partial(fused_kernel, slabs, rows, head_dim ** (-0.5)),
        out_shape=(
            jax.ShapeDtypeStruct((rows * heads, block, head_dim), low),
            jax.ShapeDtypeStruct((rows * heads, 2, block, head_dim), low),
        ),
        in_specs=[smem] * 2 + [vmem] * 4,
        out_specs=(vmem, vmem),
        scratch_shapes=[
            side,
            pltpu.VMEM((heads, rows, block, head_dim), low),
            blocks,
            pltpu.VMEM((heads, 3, TPS, keys_seen, TILE), full),
            pltpu.VMEM((heads, 3, TPS, keys_seen, TILE), full),
            pltpu.VMEM((heads, 3, TPS, TILE), full),
            pltpu.VMEM((heads, 3, 2, TPS, TILE), full),
            pltpu.VMEM((heads, 3, 2, 2, TPS, TILE), full),
            pltpu.VMEM((heads, 3, 2, TPS, TILE), full),
            pltpu.VMEM((2, tok_slab, head_dim), full),
            pltpu.VMEM((heads, rows, 2, block, head_dim), low),
            pltpu.VMEM((heads, tok_slab, head_dim), full),
            blocks,
            blocks,
            pltpu.VMEM((heads, rows, block, head_dim), low),
        ]
        + [
            pltpu.SemaphoreType.DMA((heads, 2)), pltpu.SemaphoreType.DMA((heads, 2)),
            pltpu.SemaphoreType.DMA((heads,)), pltpu.SemaphoreType.DMA((heads,)),
            pltpu.SemaphoreType.DMA((heads, 2)), pltpu.SemaphoreType.DMA((heads, 2)),
            pltpu.SemaphoreType.DMA((heads, 3, 2)), pltpu.SemaphoreType.DMA((heads, 3, 2)),
            pltpu.SemaphoreType.DMA((heads,)), pltpu.SemaphoreType.DMA((heads,)),
            pltpu.SemaphoreType.DMA((heads, 2)), pltpu.SemaphoreType.DMA((heads, 2)),
            pltpu.SemaphoreType.DMA((heads,)), pltpu.SemaphoreType.DMA((heads,)),
        ],
        compiler_params=pltpu.CompilerParams(
            collective_id=0, has_side_effects=True, vmem_limit_bytes=50 * 2**20
        ),
        cost_estimate=pl.CostEstimate(
            flops=10 * pairs * head_dim, bytes_accessed=8 * 2**20, transcendentals=pairs
        ),
    )(cols, counts, query, key, value, grad)


def on_device(slabs, rows, queries, keys, values, out_grad, col_start, valid_tiles):
    dq, dkv = fused_call(
        col_start, valid_tiles, queries.swapaxes(0, 1), keys.swapaxes(0, 1),
        values.swapaxes(0, 1), out_grad.swapaxes(0, 1), slabs, rows,
    )
    return dq.swapaxes(0, 1), dkv[:, 0].swapaxes(0, 1), dkv[:, 1].swapaxes(0, 1)


def solution(mesh):
    head_split = P("slab", "row", None)
    token_split = P(("slab", "row"), None, None)
    return jax.shard_map(
        functools.partial(on_device, mesh.shape["slab"], mesh.shape["row"]),
        mesh=mesh,
        in_specs=(head_split, head_split, head_split, token_split, P(), P()),
        out_specs=(token_split,) * 3,
        check_vma=False,
    )
```

```python
import functools

import jax
import jax.numpy as jnp
from jax import lax
from jax.experimental import pallas as pl
from jax.experimental.pallas import tpu as pltpu
from jax.sharding import PartitionSpec as P

TILE = 128
GH = 2
GW = 4
WIN_COLS = 2
TPS = 8
RUN = 8
NEG = -1e30
LOG2E = 1.4426950408889634
MESH = pl.DeviceIdType.MESH
NT = (((1,), (1,)), ((), ()))
TN = (((0,), (0,)), ((), ()))


def fused_kernel(
    slabs, rows, inv_root, cols_ref, counts_ref, q_ref, k_ref, v_ref, g_ref,
    oq_ref, okv_ref,
    q_side, g_own, g_side, expo_ref, gatt_ref, peaks, stat, stat_in, final,
    acc, kv_out, dq_own, dq_side, dq_in, dq_out,
    q_send, q_recv, a_send, a_recv, g_send, g_recv, s_send, s_recv,
    kv_send, kv_recv, dq_send, dq_recv, o_send, o_recv,
):
    heads, tok_slab, head_dim = q_ref.shape
    block = g_ref.shape[1]
    span = WIN_COLS * TILE
    row_len = GW * TILE
    slab = lax.axis_index("slab")
    row = lax.axis_index("row")
    below = lax.rem(slab + slabs - 1, slabs)
    above = lax.rem(slab + 1, slabs)
    sides = (below, above)
    half = rows // 2
    group = row // half
    mine, others = group * half, (1 - group) * half
    edges = (slab % RUN == 0, slab % RUN == RUN - 1)

    def peer(step):
        return lax.rem(row + step, rows)

    barrier = pltpu.get_barrier_semaphore()
    two_below = lax.rem(slab + slabs - 2, slabs)
    two_above = lax.rem(slab + 2, slabs)
    for side in (two_below, below, above, two_above):
        pl.semaphore_signal(barrier, inc=1, device_id=(side, row), device_id_type=MESH)

    def greet(step, carry):
        pl.semaphore_signal(barrier, inc=1, device_id=(slab, peer(step)), device_id_type=MESH)
        return carry

    lax.fori_loop(1, rows, greet, 0)
    for n in range(2):

        @pl.when(edges[n])
        def _():
            def greet_far(step, carry):
                pl.semaphore_signal(
                    barrier, inc=1, device_id=(sides[n], others + step), device_id_type=MESH
                )
                return carry

            lax.fori_loop(0, half, greet_far, 0)

    at_edge = jnp.logical_or(edges[0], edges[1])
    pl.semaphore_wait(barrier, rows + 3 + jnp.where(at_edge, half, 0))


    def to_side(src, dst, n, send, recv, head):
        return pltpu.make_async_remote_copy(
            src_ref=src,
            dst_ref=dst,
            send_sem=send.at[head, n],
            recv_sem=recv.at[head, 1 - n],
            device_id=(sides[n], row),
            device_id_type=MESH,
        )

    def from_side(ref, n, recv, head):
        pltpu.make_async_copy(ref, ref, recv.at[head, n]).wait()

    def all_sent(ref, sem):
        pltpu.make_async_copy(ref, ref, sem).wait()

    def send_queries(head):
        for n in range(2):

            @pl.when(jnp.logical_not(edges[n]))
            def _():
                to_side(q_ref.at[head], q_side.at[1 - n, head], n, q_send, q_recv, head).start()

            @pl.when(edges[n])
            def _():
                def piece(step, carry):
                    at = pl.ds(pl.multiple_of(step * block, block), block)
                    to_side(
                        q_ref.at[head, at], q_side.at[1 - n, head, at], n, q_send, q_recv, head
                    ).start()
                    return carry

                lax.fori_loop(0, rows, piece, 0)

    def spread_grad(head):
        def one(step, carry):
            other = peer(step)
            pltpu.make_async_remote_copy(
                src_ref=g_ref.at[other * heads + head],
                dst_ref=g_own.at[head, row],
                send_sem=a_send.at[head],
                recv_sem=a_recv.at[head],
                device_id=(slab, other),
                device_id_type=MESH,
            ).start()
            return carry

        lax.fori_loop(1, rows, one, 0)
        g_own[head, row] = g_ref[row * heads + head]

    def await_spread(buffer, send, recv, head):
        whole = buffer.at[pl.ds(0, rows - 1)]
        pltpu.make_async_copy(whole, whole, recv.at[head]).wait()
        pltpu.make_async_copy(whole, whole, send.at[head]).wait()

    def blocks_to_side(own, far, inbox, n, send, recv, head):
        @pl.when(jnp.logical_not(edges[n]))
        def _():
            to_side(own, inbox.at[1 - n, head], n, send, recv, head).start()

        @pl.when(edges[n])
        def _():
            def piece(step, carry):
                near = mine + step
                to_side(own.at[near], inbox.at[1 - n, head, near], n, send, recv, head).start()
                return carry

            lax.fori_loop(0, half, piece, 0)
            if far is not None:
                far(n, head)

    def far_copies(block_of, inbox, n, send, recv, head):
        def one(step, carry):
            other = others + step
            pltpu.make_async_remote_copy(
                src_ref=block_of(other),
                dst_ref=inbox.at[1 - n, head, row],
                send_sem=send.at[head, n],
                recv_sem=recv.at[head, 1 - n],
                device_id=(sides[n], other),
                device_id_type=MESH,
            ).start()
            return carry

        lax.fori_loop(0, half, one, 0)

    def spread_far(head):
        for n in range(2):

            @pl.when(edges[n])
            def _():
                far_copies(
                    lambda other: g_ref.at[other * heads + head], g_side, n, g_send, g_recv, head
                )

    def send_grads(head):
        for n in range(2):
            blocks_to_side(g_own.at[head], None, g_side, n, g_send, g_recv, head)

    def first_of(tile, part):
        owner = (below, slab, above)[part]
        return jnp.full((1, TILE), cols_ref[owner * TPS + tile], jnp.int32)

    def shift_of(tile, part):
        return (first_of(tile, part) - (tile % GW) // 2).astype(jnp.float32)

    limit = jnp.full((1, TILE), counts_ref[slab], jnp.int32)
    inside = (slab > 0, None, slab < slabs - 1)

    def bias_of(slot, tile, part):
        reach = limit if part == 1 else jnp.where(inside[part], limit, 0)
        inner = first_of(tile, part) + (slot // WIN_COLS * GW + slot % WIN_COLS)
        return jnp.where(inner < reach, 0.0, NEG)

    def pick(ref, head, tile, part):
        base = (tile % GW) // 2
        high = jnp.broadcast_to(shift_of(tile, part), (TILE, head_dim)).astype(jnp.bfloat16)
        low = 1 - high
        chosen = []
        for r in range(GH):
            cols = [
                ref[head, pl.ds(pl.multiple_of((r * GW + base + c) * TILE, TILE), TILE), :]
                for c in range(WIN_COLS + 1)
            ]
            chosen += [cols[c] * low + cols[c + 1] * high for c in range(WIN_COLS)]
        return jnp.concatenate(chosen, axis=0)

    def query_of(head, tile, part):
        at = pl.ds(pl.multiple_of(tile * TILE, TILE), TILE)
        if part == 1:
            return q_ref[head, at, :]
        return q_side[part // 2, head, at, :]

    def grad_of(head, tile, part):
        each = TILE // block
        at = pl.ds(tile * each, each)
        if part == 1:
            return g_own[head, at].reshape(TILE, head_dim)
        return g_side[part // 2, head, at].reshape(TILE, head_dim)

    def first_pass(head, part):
        def one(tile, carry):
            keys = pick(k_ref, head, tile, part)
            values = pick(v_ref, head, tile, part)
            bias = jnp.concatenate(
                [
                    jnp.broadcast_to(bias_of(n, tile, part), (TILE, TILE))
                    for n in range(GH * WIN_COLS)
                ],
                axis=0,
            )
            scores = lax.dot_general(
                keys, query_of(head, tile, part), NT, preferred_element_type=jnp.float32
            )
            scores = scores * (inv_root * LOG2E) + bias
            peak = jnp.max(scores, axis=0, keepdims=True)
            expo = jnp.exp2(scores - peak)
            grad_attend = lax.dot_general(
                values, grad_of(head, tile, part), NT, preferred_element_type=jnp.float32
            )
            expo_ref[head, part, tile] = expo
            gatt_ref[head, part, tile] = grad_attend
            at = pl.ds(tile, 1)
            total = jnp.sum(expo, axis=0, keepdims=True)
            dot = jnp.sum(expo * grad_attend, axis=0, keepdims=True)
            peaks[head, part, at, :] = peak
            stat[head, part, 0, at, :] = peak + jnp.log2(total)
            stat[head, part, 1, at, :] = dot / total
            return carry

        lax.fori_loop(0, TPS, one, 0)

    routes = (
        (1, above, 0, 0), (2, two_above, 0, 1), (0, below, 1, 0),
        (2, above, 1, 1), (0, two_below, 2, 0), (1, below, 2, 1),
    )

    def stat_copy(head, route):
        part, target, there, slot = route
        return pltpu.make_async_remote_copy(
            src_ref=stat.at[head, part],
            dst_ref=stat_in.at[head, there, slot],
            send_sem=s_send.at[head, there, slot],
            recv_sem=s_recv.at[head, there, slot],
            device_id=(target, row),
            device_id_type=MESH,
        )

    def send_stats(head):
        for route in routes:
            stat_copy(head, route).start()

    def combine(head, part):
        for slot in range(2):
            ref = stat_in.at[head, part, slot]
            pltpu.make_async_copy(ref, ref, s_recv.at[head, part, slot]).wait()
        logs = [stat[head, part, 0], stat_in[head, part, 0, 0], stat_in[head, part, 1, 0]]
        dots = [stat[head, part, 1], stat_in[head, part, 0, 1], stat_in[head, part, 1, 1]]
        top = jnp.maximum(jnp.maximum(logs[0], logs[1]), logs[2])
        weights = [jnp.exp2(one - top) for one in logs]
        total = weights[0] + weights[1] + weights[2]
        final[head, part, 0] = jnp.exp2(peaks[head, part] - top) / total
        final[head, part, 1] = (
            weights[0] * dots[0] + weights[1] * dots[1] + weights[2] * dots[2]
        ) / total

    def second_pass(head, part):
        def one(tile, carry):
            base = (tile % GW) // 2
            at = pl.ds(tile, 1)
            shifted = jnp.broadcast_to(shift_of(tile, part), (TILE, head_dim)) > 0.5
            keys = pick(k_ref, head, tile, part)
            attend = expo_ref[head, part, tile] * final[head, part, 0, at, :]
            grad_scores = attend * (gatt_ref[head, part, tile] - final[head, part, 1, at, :])
            grad_scores = grad_scores.astype(jnp.bfloat16)
            attend_b = attend.astype(jnp.bfloat16)
            dq = lax.dot_general(grad_scores, keys, TN, preferred_element_type=jnp.float32)
            rows_at = pl.ds(pl.multiple_of(tile * TILE, TILE), TILE)
            if part == 1:
                dq_own[head, rows_at, :] = dq * inv_root
            else:
                each = TILE // block
                dq_side[part // 2, head, pl.ds(tile * each, each)] = (
                    (dq * inv_root).astype(jnp.bfloat16).reshape(each, block, head_dim)
                )
            dk = jnp.dot(
                grad_scores, query_of(head, tile, part), preferred_element_type=jnp.float32
            )
            dv = jnp.dot(
                attend_b, grad_of(head, tile, part), preferred_element_type=jnp.float32
            )
            for which, term in ((0, dk), (1, dv)):
                for r in range(GH):
                    near = term[r * span : r * span + TILE]
                    far = term[r * span + TILE : (r + 1) * span]
                    adds = (
                        jnp.where(shifted, 0.0, near),
                        jnp.where(shifted, near, far),
                        jnp.where(shifted, far, 0.0),
                    )
                    for col, add in enumerate(adds):
                        where = pl.ds(
                            pl.multiple_of((r * GW + base + col) * TILE, TILE), TILE
                        )
                        acc[which, where, :] += add
            return carry

        lax.fori_loop(0, TPS, one, 0)

    def send_home(head):
        def stage(other, carry):
            at = pl.ds(pl.multiple_of(other * block, block), block)
            kv_out[head, other, 0] = (acc[0, at, :] * inv_root).astype(jnp.bfloat16)
            kv_out[head, other, 1] = acc[1, at, :].astype(jnp.bfloat16)
            return carry

        lax.fori_loop(0, rows, stage, 0)

        def one(step, carry):
            other = peer(step)
            pltpu.make_async_remote_copy(
                src_ref=kv_out.at[head, other],
                dst_ref=okv_ref.at[row * heads + head],
                send_sem=kv_send.at[head],
                recv_sem=kv_recv.at[head],
                device_id=(slab, other),
                device_id_type=MESH,
            ).start()
            return carry

        lax.fori_loop(1, rows, one, 0)
        okv_ref[row * heads + head] = kv_out[head, row]

    def send_dq(head, n):
        def far(n, head):
            far_copies(
                lambda other: dq_side.at[n, head, other], dq_in, n, dq_send, dq_recv, head
            )

        blocks_to_side(dq_side.at[n, head], far, dq_in, n, dq_send, dq_recv, head)

    def finish_dq(head):
        for n in range(2):
            from_side(dq_in.at[n, head], n, dq_recv, head)

        def stage(other, carry):
            at = pl.ds(pl.multiple_of(other * block, block), block)
            total = dq_own[head, at, :]
            for n in range(2):
                here = jnp.logical_or(jnp.logical_not(edges[n]), other // half == group)
                total += jnp.where(here, dq_in[n, head, other].astype(jnp.float32), 0.0)
            dq_out[head, other] = total.astype(jnp.bfloat16)
            return carry

        lax.fori_loop(0, rows, stage, 0)

        def one(step, carry):
            other = peer(step)
            pltpu.make_async_remote_copy(
                src_ref=dq_out.at[head, other],
                dst_ref=oq_ref.at[row * heads + head],
                send_sem=o_send.at[head],
                recv_sem=o_recv.at[head],
                device_id=(slab, other),
                device_id_type=MESH,
            ).start()
            return carry

        lax.fori_loop(1, rows, one, 0)
        oq_ref[row * heads + head] = dq_out[head, row]

    def sides_pass(head):
        for n in range(2):
            from_side(q_side.at[n, head], n, q_recv, head)
            from_side(g_side.at[n, head], n, g_recv, head)
            first_pass(head, 2 * n)
        send_stats(head)

    def results(head):
        acc[...] = jnp.zeros_like(acc)
        for n in range(2):
            combine(head, 2 * n)
            second_pass(head, 2 * n)
            send_dq(head, n)
        combine(head, 1)
        second_pass(head, 1)
        send_home(head)

    for head in range(heads):
        spread_far(head)
        spread_grad(head)
    for head in range(heads):
        send_queries(head)
    await_spread(g_own.at[0], a_send, a_recv, 0)
    send_grads(0)
    first_pass(0, 1)
    await_spread(g_own.at[1], a_send, a_recv, 1)
    send_grads(1)
    sides_pass(0)
    first_pass(1, 1)
    sides_pass(1)
    results(0)
    results(1)
    for head in range(heads):
        finish_dq(head)

    for head in range(heads):
        for n in range(2):
            to_side(q_ref.at[head], q_side.at[1 - n, head], n, q_send, q_recv, head).wait_send()
            to_side(g_own.at[head], g_side.at[1 - n, head], n, g_send, g_recv, head).wait_send()
            to_side(dq_side.at[n, head], dq_in.at[1 - n, head], n, dq_send, dq_recv, head).wait_send()
        for route in routes:
            stat_copy(head, route).wait_send()
        await_spread(kv_out.at[head], kv_send, kv_recv, head)
    for head in range(heads):
        await_spread(dq_out.at[head], o_send, o_recv, head)
        for n in range(2):

            @pl.when(edges[n])
            def _():
                def add(step, carry):
                    other = others + step
                    at = other * heads + head
                    total = oq_ref[at].astype(jnp.float32) + dq_in[n, head, other].astype(jnp.float32)
                    oq_ref[at] = total.astype(jnp.bfloat16)
                    return carry

                lax.fori_loop(0, half, add, 0)


def fused_call(cols, counts, query, key, value, grad, slabs, rows):
    heads, tok_slab, head_dim = query.shape
    block = grad.shape[1]
    vmem = pl.BlockSpec(memory_space=pltpu.VMEM)
    smem = pl.BlockSpec(memory_space=pltpu.SMEM)
    keys_seen = GH * WIN_COLS * TILE
    pairs = heads * tok_slab * 3 * keys_seen
    low, full = jnp.bfloat16, jnp.float32
    side = pltpu.VMEM((2, heads, tok_slab, head_dim), low)
    blocks = pltpu.VMEM((2, heads, rows, block, head_dim), low)
    return pl.pallas_call(
        functools.partial(fused_kernel, slabs, rows, head_dim ** (-0.5)),
        out_shape=(
            jax.ShapeDtypeStruct((rows * heads, block, head_dim), low),
            jax.ShapeDtypeStruct((rows * heads, 2, block, head_dim), low),
        ),
        in_specs=[smem] * 2 + [vmem] * 4,
        out_specs=(vmem, vmem),
        scratch_shapes=[
            side,
            pltpu.VMEM((heads, rows, block, head_dim), low),
            blocks,
            pltpu.VMEM((heads, 3, TPS, keys_seen, TILE), full),
            pltpu.VMEM((heads, 3, TPS, keys_seen, TILE), full),
            pltpu.VMEM((heads, 3, TPS, TILE), full),
            pltpu.VMEM((heads, 3, 2, TPS, TILE), full),
            pltpu.VMEM((heads, 3, 2, 2, TPS, TILE), full),
            pltpu.VMEM((heads, 3, 2, TPS, TILE), full),
            pltpu.VMEM((2, tok_slab, head_dim), full),
            pltpu.VMEM((heads, rows, 2, block, head_dim), low),
            pltpu.VMEM((heads, tok_slab, head_dim), full),
            blocks,
            blocks,
            pltpu.VMEM((heads, rows, block, head_dim), low),
        ]
        + [
            pltpu.SemaphoreType.DMA((heads, 2)), pltpu.SemaphoreType.DMA((heads, 2)),
            pltpu.SemaphoreType.DMA((heads,)), pltpu.SemaphoreType.DMA((heads,)),
            pltpu.SemaphoreType.DMA((heads, 2)), pltpu.SemaphoreType.DMA((heads, 2)),
            pltpu.SemaphoreType.DMA((heads, 3, 2)), pltpu.SemaphoreType.DMA((heads, 3, 2)),
            pltpu.SemaphoreType.DMA((heads,)), pltpu.SemaphoreType.DMA((heads,)),
            pltpu.SemaphoreType.DMA((heads, 2)), pltpu.SemaphoreType.DMA((heads, 2)),
            pltpu.SemaphoreType.DMA((heads,)), pltpu.SemaphoreType.DMA((heads,)),
        ],
        compiler_params=pltpu.CompilerParams(
            collective_id=0, has_side_effects=True, vmem_limit_bytes=50 * 2**20
        ),
        cost_estimate=pl.CostEstimate(
            flops=10 * pairs * head_dim, bytes_accessed=8 * 2**20, transcendentals=pairs
        ),
    )(cols, counts, query, key, value, grad)


def on_device(slabs, rows, queries, keys, values, out_grad, col_start, valid_tiles):
    dq, dkv = fused_call(
        col_start, valid_tiles, queries.swapaxes(0, 1), keys.swapaxes(0, 1),
        values.swapaxes(0, 1), out_grad.swapaxes(0, 1), slabs, rows,
    )
    return dq.swapaxes(0, 1), dkv[:, 0].swapaxes(0, 1), dkv[:, 1].swapaxes(0, 1)


def solution(mesh):
    head_split = P("slab", "row", None)
    token_split = P(("slab", "row"), None, None)
    return jax.shard_map(
        functools.partial(on_device, mesh.shape["slab"], mesh.shape["row"]),
        mesh=mesh,
        in_specs=(head_split, head_split, head_split, token_split, P(), P()),
        out_specs=(token_split,) * 3,
        check_vma=False,
    )
```

```python
import functools

import jax
import jax.numpy as jnp
from jax import lax
from jax.experimental import pallas as pl
from jax.experimental.pallas import tpu as pltpu
from jax.sharding import PartitionSpec as P

TILE = 128
GH = 2
GW = 4
WIN_COLS = 2
TPS = 8
RUN = 8
NEG = -1e30
LOG2E = 1.4426950408889634
MESH = pl.DeviceIdType.MESH
NT = (((1,), (1,)), ((), ()))
TN = (((0,), (0,)), ((), ()))


def fused_kernel(
    slabs, rows, inv_root, cols_ref, counts_ref, q_ref, k_ref, v_ref, g_ref,
    oq_ref, okv_ref,
    q_side, g_own, g_side, expo_ref, gatt_ref, peaks, stat, stat_in, final,
    acc, kv_out, dq_own, dq_side, dq_in, dq_out,
    q_send, q_recv, a_send, a_recv, g_send, g_recv, s_send, s_recv,
    kv_send, kv_recv, dq_send, dq_recv, o_send, o_recv,
):
    heads, tok_slab, head_dim = q_ref.shape
    block = g_ref.shape[1]
    span = WIN_COLS * TILE
    row_len = GW * TILE
    slab = lax.axis_index("slab")
    row = lax.axis_index("row")
    below = lax.rem(slab + slabs - 1, slabs)
    above = lax.rem(slab + 1, slabs)
    sides = (below, above)
    half = rows // 2
    group = row // half
    mine, others = group * half, (1 - group) * half
    edges = (slab % RUN == 0, slab % RUN == RUN - 1)

    def peer(step):
        return lax.rem(row + step, rows)

    barrier = pltpu.get_barrier_semaphore()
    two_below = lax.rem(slab + slabs - 2, slabs)
    two_above = lax.rem(slab + 2, slabs)
    for side in (two_below, below, above, two_above):
        pl.semaphore_signal(barrier, inc=1, device_id=(side, row), device_id_type=MESH)

    def greet(step, carry):
        pl.semaphore_signal(barrier, inc=1, device_id=(slab, peer(step)), device_id_type=MESH)
        return carry

    lax.fori_loop(1, rows, greet, 0)
    for n in range(2):

        @pl.when(edges[n])
        def _():
            def greet_far(step, carry):
                pl.semaphore_signal(
                    barrier, inc=1, device_id=(sides[n], others + step), device_id_type=MESH
                )
                return carry

            lax.fori_loop(0, half, greet_far, 0)

    at_edge = jnp.logical_or(edges[0], edges[1])
    pl.semaphore_wait(barrier, rows + 3 + jnp.where(at_edge, half, 0))


    def to_side(src, dst, n, send, recv, head):
        return pltpu.make_async_remote_copy(
            src_ref=src,
            dst_ref=dst,
            send_sem=send.at[head, n],
            recv_sem=recv.at[head, 1 - n],
            device_id=(sides[n], row),
            device_id_type=MESH,
        )

    def from_side(ref, n, recv, head):
        pltpu.make_async_copy(ref, ref, recv.at[head, n]).wait()

    def all_sent(ref, sem):
        pltpu.make_async_copy(ref, ref, sem).wait()

    def send_queries(head):
        for n in range(2):
            to_side(q_ref.at[head], q_side.at[1 - n, head], n, q_send, q_recv, head).start()

    def spread_grad(head):
        def one(step, carry):
            other = peer(step)
            pltpu.make_async_remote_copy(
                src_ref=g_ref.at[other * heads + head],
                dst_ref=g_own.at[head, row],
                send_sem=a_send.at[head],
                recv_sem=a_recv.at[head],
                device_id=(slab, other),
                device_id_type=MESH,
            ).start()
            return carry

        lax.fori_loop(1, rows, one, 0)
        g_own[head, row] = g_ref[row * heads + head]

    def await_spread(buffer, send, recv, head):
        whole = buffer.at[pl.ds(0, rows - 1)]
        pltpu.make_async_copy(whole, whole, recv.at[head]).wait()
        pltpu.make_async_copy(whole, whole, send.at[head]).wait()

    def blocks_to_side(own, far, inbox, n, send, recv, head):
        @pl.when(jnp.logical_not(edges[n]))
        def _():
            to_side(own, inbox.at[1 - n, head], n, send, recv, head).start()

        @pl.when(edges[n])
        def _():
            near = pl.ds(mine, half)
            to_side(own.at[near], inbox.at[1 - n, head, near], n, send, recv, head).start()
            if far is not None:
                far(n, head)

    def far_copies(block_of, inbox, n, send, recv, head):
        def one(step, carry):
            other = others + step
            pltpu.make_async_remote_copy(
                src_ref=block_of(other),
                dst_ref=inbox.at[1 - n, head, row],
                send_sem=send.at[head, n],
                recv_sem=recv.at[head, 1 - n],
                device_id=(sides[n], other),
                device_id_type=MESH,
            ).start()
            return carry

        lax.fori_loop(0, half, one, 0)

    def spread_far(head):
        for n in range(2):

            @pl.when(edges[n])
            def _():
                far_copies(
                    lambda other: g_ref.at[other * heads + head], g_side, n, g_send, g_recv, head
                )

    def send_grads(head):
        for n in range(2):
            blocks_to_side(g_own.at[head], None, g_side, n, g_send, g_recv, head)

    def first_of(tile, part):
        owner = (below, slab, above)[part]
        return jnp.full((1, TILE), cols_ref[owner * TPS + tile], jnp.int32)

    def shift_of(tile, part):
        return (first_of(tile, part) - (tile % GW) // 2).astype(jnp.float32)

    limit = jnp.full((1, TILE), counts_ref[slab], jnp.int32)
    inside = (slab > 0, None, slab < slabs - 1)

    def bias_of(slot, tile, part):
        reach = limit if part == 1 else jnp.where(inside[part], limit, 0)
        inner = first_of(tile, part) + (slot // WIN_COLS * GW + slot % WIN_COLS)
        return jnp.where(inner < reach, 0.0, NEG)

    def pick(ref, head, tile, part):
        base = (tile % GW) // 2
        high = jnp.broadcast_to(shift_of(tile, part), (TILE, head_dim)).astype(jnp.bfloat16)
        low = 1 - high
        chosen = []
        for r in range(GH):
            cols = [
                ref[head, pl.ds(pl.multiple_of((r * GW + base + c) * TILE, TILE), TILE), :]
                for c in range(WIN_COLS + 1)
            ]
            chosen += [cols[c] * low + cols[c + 1] * high for c in range(WIN_COLS)]
        return jnp.concatenate(chosen, axis=0)

    def query_of(head, tile, part):
        at = pl.ds(pl.multiple_of(tile * TILE, TILE), TILE)
        if part == 1:
            return q_ref[head, at, :]
        return q_side[part // 2, head, at, :]

    def grad_of(head, tile, part):
        each = TILE // block
        at = pl.ds(tile * each, each)
        if part == 1:
            return g_own[head, at].reshape(TILE, head_dim)
        return g_side[part // 2, head, at].reshape(TILE, head_dim)

    def first_pass(head, part):
        def one(tile, carry):
            keys = pick(k_ref, head, tile, part)
            values = pick(v_ref, head, tile, part)
            bias = jnp.concatenate(
                [
                    jnp.broadcast_to(bias_of(n, tile, part), (TILE, TILE))
                    for n in range(GH * WIN_COLS)
                ],
                axis=0,
            )
            scores = lax.dot_general(
                keys, query_of(head, tile, part), NT, preferred_element_type=jnp.float32
            )
            scores = scores * (inv_root * LOG2E) + bias
            peak = jnp.max(scores, axis=0, keepdims=True)
            expo = jnp.exp2(scores - peak)
            grad_attend = lax.dot_general(
                values, grad_of(head, tile, part), NT, preferred_element_type=jnp.float32
            )
            expo_ref[head, part, tile] = expo
            gatt_ref[head, part, tile] = grad_attend
            at = pl.ds(tile, 1)
            total = jnp.sum(expo, axis=0, keepdims=True)
            dot = jnp.sum(expo * grad_attend, axis=0, keepdims=True)
            peaks[head, part, at, :] = peak
            stat[head, part, 0, at, :] = peak + jnp.log2(total)
            stat[head, part, 1, at, :] = dot / total
            return carry

        lax.fori_loop(0, TPS, one, 0)

    routes = (
        (1, above, 0, 0), (2, two_above, 0, 1), (0, below, 1, 0),
        (2, above, 1, 1), (0, two_below, 2, 0), (1, below, 2, 1),
    )

    def stat_copy(head, route):
        part, target, there, slot = route
        return pltpu.make_async_remote_copy(
            src_ref=stat.at[head, part],
            dst_ref=stat_in.at[head, there, slot],
            send_sem=s_send.at[head, there, slot],
            recv_sem=s_recv.at[head, there, slot],
            device_id=(target, row),
            device_id_type=MESH,
        )

    def send_stats(head):
        for route in routes:
            stat_copy(head, route).start()

    def combine(head, part):
        for slot in range(2):
            ref = stat_in.at[head, part, slot]
            pltpu.make_async_copy(ref, ref, s_recv.at[head, part, slot]).wait()
        logs = [stat[head, part, 0], stat_in[head, part, 0, 0], stat_in[head, part, 1, 0]]
        dots = [stat[head, part, 1], stat_in[head, part, 0, 1], stat_in[head, part, 1, 1]]
        top = jnp.maximum(jnp.maximum(logs[0], logs[1]), logs[2])
        weights = [jnp.exp2(one - top) for one in logs]
        total = weights[0] + weights[1] + weights[2]
        final[head, part, 0] = jnp.exp2(peaks[head, part] - top) / total
        final[head, part, 1] = (
            weights[0] * dots[0] + weights[1] * dots[1] + weights[2] * dots[2]
        ) / total

    def second_pass(head, part):
        def one(tile, carry):
            base = (tile % GW) // 2
            at = pl.ds(tile, 1)
            shifted = jnp.broadcast_to(shift_of(tile, part), (TILE, head_dim)) > 0.5
            keys = pick(k_ref, head, tile, part)
            attend = expo_ref[head, part, tile] * final[head, part, 0, at, :]
            grad_scores = attend * (gatt_ref[head, part, tile] - final[head, part, 1, at, :])
            grad_scores = grad_scores.astype(jnp.bfloat16)
            attend_b = attend.astype(jnp.bfloat16)
            dq = lax.dot_general(grad_scores, keys, TN, preferred_element_type=jnp.float32)
            rows_at = pl.ds(pl.multiple_of(tile * TILE, TILE), TILE)
            if part == 1:
                dq_own[head, rows_at, :] = dq * inv_root
            else:
                each = TILE // block
                dq_side[part // 2, head, pl.ds(tile * each, each)] = (
                    (dq * inv_root).astype(jnp.bfloat16).reshape(each, block, head_dim)
                )
            dk = jnp.dot(
                grad_scores, query_of(head, tile, part), preferred_element_type=jnp.float32
            )
            dv = jnp.dot(
                attend_b, grad_of(head, tile, part), preferred_element_type=jnp.float32
            )
            for which, term in ((0, dk), (1, dv)):
                for r in range(GH):
                    near = term[r * span : r * span + TILE]
                    far = term[r * span + TILE : (r + 1) * span]
                    adds = (
                        jnp.where(shifted, 0.0, near),
                        jnp.where(shifted, near, far),
                        jnp.where(shifted, far, 0.0),
                    )
                    for col, add in enumerate(adds):
                        where = pl.ds(
                            pl.multiple_of((r * GW + base + col) * TILE, TILE), TILE
                        )
                        acc[which, where, :] += add
            return carry

        lax.fori_loop(0, TPS, one, 0)

    def send_home(head):
        def stage(other, carry):
            at = pl.ds(pl.multiple_of(other * block, block), block)
            kv_out[head, other, 0] = (acc[0, at, :] * inv_root).astype(jnp.bfloat16)
            kv_out[head, other, 1] = acc[1, at, :].astype(jnp.bfloat16)
            return carry

        lax.fori_loop(0, rows, stage, 0)

        def one(step, carry):
            other = peer(step)
            pltpu.make_async_remote_copy(
                src_ref=kv_out.at[head, other],
                dst_ref=okv_ref.at[row * heads + head],
                send_sem=kv_send.at[head],
                recv_sem=kv_recv.at[head],
                device_id=(slab, other),
                device_id_type=MESH,
            ).start()
            return carry

        lax.fori_loop(1, rows, one, 0)
        okv_ref[row * heads + head] = kv_out[head, row]

    def send_dq(head, n):
        def far(n, head):
            far_copies(
                lambda other: dq_side.at[n, head, other], dq_in, n, dq_send, dq_recv, head
            )

        blocks_to_side(dq_side.at[n, head], far, dq_in, n, dq_send, dq_recv, head)

    def finish_dq(head):
        for n in range(2):
            from_side(dq_in.at[n, head], n, dq_recv, head)

        def stage(other, carry):
            at = pl.ds(pl.multiple_of(other * block, block), block)
            total = dq_own[head, at, :]
            for n in range(2):
                here = jnp.logical_or(jnp.logical_not(edges[n]), other // half == group)
                total += jnp.where(here, dq_in[n, head, other].astype(jnp.float32), 0.0)
            dq_out[head, other] = total.astype(jnp.bfloat16)
            return carry

        lax.fori_loop(0, rows, stage, 0)

        def one(step, carry):
            other = peer(step)
            pltpu.make_async_remote_copy(
                src_ref=dq_out.at[head, other],
                dst_ref=oq_ref.at[row * heads + head],
                send_sem=o_send.at[head],
                recv_sem=o_recv.at[head],
                device_id=(slab, other),
                device_id_type=MESH,
            ).start()
            return carry

        lax.fori_loop(1, rows, one, 0)
        oq_ref[row * heads + head] = dq_out[head, row]

    def sides_pass(head):
        for n in range(2):
            from_side(q_side.at[n, head], n, q_recv, head)
            from_side(g_side.at[n, head], n, g_recv, head)
            first_pass(head, 2 * n)
        send_stats(head)

    def results(head):
        acc[...] = jnp.zeros_like(acc)
        for n in range(2):
            combine(head, 2 * n)
            second_pass(head, 2 * n)
            send_dq(head, n)
        combine(head, 1)
        second_pass(head, 1)

    for head in range(heads):
        spread_far(head)
        spread_grad(head)
    for head in range(heads):
        send_queries(head)
    await_spread(g_own.at[0], a_send, a_recv, 0)
    send_grads(0)
    first_pass(0, 1)
    await_spread(g_own.at[1], a_send, a_recv, 1)
    send_grads(1)
    sides_pass(0)
    first_pass(1, 1)
    sides_pass(1)
    results(0)
    send_home(0)
    results(1)
    for head in range(heads):
        finish_dq(head)
    send_home(1)

    for head in range(heads):
        for n in range(2):
            to_side(q_ref.at[head], q_side.at[1 - n, head], n, q_send, q_recv, head).wait_send()
            to_side(g_own.at[head], g_side.at[1 - n, head], n, g_send, g_recv, head).wait_send()
            to_side(dq_side.at[n, head], dq_in.at[1 - n, head], n, dq_send, dq_recv, head).wait_send()
        for route in routes:
            stat_copy(head, route).wait_send()
        await_spread(kv_out.at[head], kv_send, kv_recv, head)
    for head in range(heads):
        await_spread(dq_out.at[head], o_send, o_recv, head)
        for n in range(2):

            @pl.when(edges[n])
            def _():
                def add(step, carry):
                    other = others + step
                    at = other * heads + head
                    total = oq_ref[at].astype(jnp.float32) + dq_in[n, head, other].astype(jnp.float32)
                    oq_ref[at] = total.astype(jnp.bfloat16)
                    return carry

                lax.fori_loop(0, half, add, 0)


def fused_call(cols, counts, query, key, value, grad, slabs, rows):
    heads, tok_slab, head_dim = query.shape
    block = grad.shape[1]
    vmem = pl.BlockSpec(memory_space=pltpu.VMEM)
    smem = pl.BlockSpec(memory_space=pltpu.SMEM)
    keys_seen = GH * WIN_COLS * TILE
    pairs = heads * tok_slab * 3 * keys_seen
    low, full = jnp.bfloat16, jnp.float32
    side = pltpu.VMEM((2, heads, tok_slab, head_dim), low)
    blocks = pltpu.VMEM((2, heads, rows, block, head_dim), low)
    return pl.pallas_call(
        functools.partial(fused_kernel, slabs, rows, head_dim ** (-0.5)),
        out_shape=(
            jax.ShapeDtypeStruct((rows * heads, block, head_dim), low),
            jax.ShapeDtypeStruct((rows * heads, 2, block, head_dim), low),
        ),
        in_specs=[smem] * 2 + [vmem] * 4,
        out_specs=(vmem, vmem),
        scratch_shapes=[
            side,
            pltpu.VMEM((heads, rows, block, head_dim), low),
            blocks,
            pltpu.VMEM((heads, 3, TPS, keys_seen, TILE), full),
            pltpu.VMEM((heads, 3, TPS, keys_seen, TILE), full),
            pltpu.VMEM((heads, 3, TPS, TILE), full),
            pltpu.VMEM((heads, 3, 2, TPS, TILE), full),
            pltpu.VMEM((heads, 3, 2, 2, TPS, TILE), full),
            pltpu.VMEM((heads, 3, 2, TPS, TILE), full),
            pltpu.VMEM((2, tok_slab, head_dim), full),
            pltpu.VMEM((heads, rows, 2, block, head_dim), low),
            pltpu.VMEM((heads, tok_slab, head_dim), full),
            blocks,
            blocks,
            pltpu.VMEM((heads, rows, block, head_dim), low),
        ]
        + [
            pltpu.SemaphoreType.DMA((heads, 2)), pltpu.SemaphoreType.DMA((heads, 2)),
            pltpu.SemaphoreType.DMA((heads,)), pltpu.SemaphoreType.DMA((heads,)),
            pltpu.SemaphoreType.DMA((heads, 2)), pltpu.SemaphoreType.DMA((heads, 2)),
            pltpu.SemaphoreType.DMA((heads, 3, 2)), pltpu.SemaphoreType.DMA((heads, 3, 2)),
            pltpu.SemaphoreType.DMA((heads,)), pltpu.SemaphoreType.DMA((heads,)),
            pltpu.SemaphoreType.DMA((heads, 2)), pltpu.SemaphoreType.DMA((heads, 2)),
            pltpu.SemaphoreType.DMA((heads,)), pltpu.SemaphoreType.DMA((heads,)),
        ],
        compiler_params=pltpu.CompilerParams(
            collective_id=0, has_side_effects=True, vmem_limit_bytes=50 * 2**20
        ),
        cost_estimate=pl.CostEstimate(
            flops=10 * pairs * head_dim, bytes_accessed=8 * 2**20, transcendentals=pairs
        ),
    )(cols, counts, query, key, value, grad)


def on_device(slabs, rows, queries, keys, values, out_grad, col_start, valid_tiles):
    dq, dkv = fused_call(
        col_start, valid_tiles, queries.swapaxes(0, 1), keys.swapaxes(0, 1),
        values.swapaxes(0, 1), out_grad.swapaxes(0, 1), slabs, rows,
    )
    return dq.swapaxes(0, 1), dkv[:, 0].swapaxes(0, 1), dkv[:, 1].swapaxes(0, 1)


def solution(mesh):
    head_split = P("slab", "row", None)
    token_split = P(("slab", "row"), None, None)
    return jax.shard_map(
        functools.partial(on_device, mesh.shape["slab"], mesh.shape["row"]),
        mesh=mesh,
        in_specs=(head_split, head_split, head_split, token_split, P(), P()),
        out_specs=(token_split,) * 3,
        check_vma=False,
    )
```
